128 devices in a mesh: depth: 4 (over y), screen: 32 (over z, x, core).
Axes of the slice: x: 4, y: 4, z: 4, core: 2. Of those that a mesh axis runs over, the one named last changes fastest.
Arguments:
- brick_field: float32 [4, 32, 32, 128, 128], P('depth', 'screen'), may hold values from 0 to 1
- tf_color: bfloat16 [3, 128], replicated, may hold values from 0 to 1
- tf_extinction: bfloat16 [128], replicated, may hold values from 0.0019989014 to 0.049804688
- brick_map: int32 [128], replicated, may hold values from 0 to 127, as said below
- view_order: int32 [128], replicated, may hold values from 0 to 127, as said below
- anchors: int32 [128, 2], replicated, may hold values from 0 to 896, as said below
- rects: int32 [128, 4], replicated, may hold values from 0 to 128, as said below
Outputs:
- frame_image: float32 [4, 512, 1024], P(None, None, 'depth')
The draws below stay inside these ranges and needn't reach their ends.
Inputs may be any that keep to these rules, and one draw needn't show every extreme that they name: `brick_map`: a permutation of the brick numbers. `view_order`: a permutation of the brick numbers. Reading each brick's rank through brick_map, the slot ranks are the front-to-back order of a binary tree over the slots numbered l * 32 + c: each inner node covers an aligned run of slot numbers of power-of-two length and visits its lower half or its upper half first. `anchors`: rows from 0 to 384, columns from 0 to 896; both ends reached on both. `rects`: first row below end row, both within 0 .. 128; first column below end column, both within 0 .. 128.
All inputs are finite; a program needn't handle non-finite values.
Results may differ from the reference program's by a relative error of at most 0.00039.
Values sent between devices are 32-bit elements; how exact they have to be, the bound alone decides.
A program may use at most 128 MiB of HBM per device.

```python
import math
import jax
import jax.numpy as jnp
from jax import lax

IMG_W = 1024
IMG_H = 512
FOOT_H = 128
FOOT_W = 128
SAMPLES = 32
KNOTS = 128
LAYERS = 4
COLUMNS = 32
BRICKS = 128


def arrangement(key):
    map_key = jax.random.fold_in(key, 11)
    flip_key = jax.random.fold_in(key, 12)
    brick_ids = jax.random.permutation(map_key, BRICKS).astype(jnp.int32)
    flip_bits = jax.random.randint(flip_key, (BRICKS,), 0, 2, dtype=jnp.int32)
    slot_index = jnp.arange(BRICKS, dtype=jnp.int32)
    levels = BRICKS.bit_length() - 1
    leaf_rank = jnp.zeros((BRICKS,), jnp.int32)
    for level_index in range(levels):
        shift_by = levels - 1 - level_index
        node_index = (1 << level_index) + jnp.right_shift(slot_index, shift_by + 1)
        bit_value = jnp.bitwise_and(jnp.right_shift(slot_index, shift_by), 1)
        turned = jnp.bitwise_xor(bit_value, flip_bits[node_index])
        leaf_rank = leaf_rank + jnp.left_shift(turned, shift_by)
    ordering = jnp.zeros((BRICKS,), jnp.int32).at[leaf_rank].set(brick_ids)
    return (brick_ids, ordering)


def draw_brick_map(key, part):
    return arrangement(key)[0]


def draw_view_order(key, part):
    return arrangement(key)[1]


def draw_anchors(key, part):
    key = jax.random.fold_in(key, 3)
    row_key, col_key, pick_key = jax.random.split(key, 3)
    row_start = jax.random.randint(row_key, (BRICKS,), 0, IMG_H - FOOT_H + 1, dtype=jnp.int32)
    col_start = jax.random.randint(col_key, (BRICKS,), 0, IMG_W - FOOT_W + 1, dtype=jnp.int32)
    chosen = jax.random.permutation(pick_key, BRICKS)[:2]
    row_start = row_start.at[chosen[0]].set(0).at[chosen[1]].set(IMG_H - FOOT_H)
    col_start = col_start.at[chosen[0]].set(0).at[chosen[1]].set(IMG_W - FOOT_W)
    return jnp.stack([row_start, col_start], axis=1).astype(jnp.int32)


def draw_rects(key, part):
    key = jax.random.fold_in(key, 5)
    first_key, second_key, third_key, fourth_key, pick_key = jax.random.split(key, 5)
    row_first = jax.random.randint(first_key, (BRICKS,), 0, FOOT_H // 4 + 1, dtype=jnp.int32)
    row_end = jax.random.randint(second_key, (BRICKS,), FOOT_H - FOOT_H // 4, FOOT_H + 1, dtype=jnp.int32)
    col_first = jax.random.randint(third_key, (BRICKS,), 0, FOOT_W // 4 + 1, dtype=jnp.int32)
    col_end = jax.random.randint(fourth_key, (BRICKS,), FOOT_W - FOOT_W // 4, FOOT_W + 1, dtype=jnp.int32)
    chosen = jax.random.randint(pick_key, (), 0, BRICKS, dtype=jnp.int32)
    row_first = row_first.at[chosen].set(0)
    row_end = row_end.at[chosen].set(FOOT_H)
    col_first = col_first.at[chosen].set(0)
    col_end = col_end.at[chosen].set(FOOT_W)
    return jnp.stack([row_first, row_end, col_first, col_end], axis=1).astype(jnp.int32)


def level_of(key, shape, shards, low, largest):
    loudness, own = 1.0, jax.random.fold_in(key, 6)
    for dim, parts in shards:
        draws = jnp.exp(jax.random.uniform(jax.random.fold_in(own, dim), (parts,), jnp.float32, low / len(shards), largest / len(shards)))
        loudness = loudness * jnp.repeat(draws, shape[dim] // parts).reshape([-1 if axis == dim else 1 for axis in range(len(shape))])
    return loudness


def setup_inputs(seed: int = 0) -> dict:
    arg_keys = jax.random.split(jax.random.key(seed), 8)
    return {
        "brick_field": jnp.clip(1.0 * jax.random.uniform(arg_keys[0], (LAYERS, COLUMNS, SAMPLES, FOOT_H, FOOT_W), jnp.float32) ** level_of(arg_keys[0], (LAYERS, COLUMNS, SAMPLES, FOOT_H, FOOT_W), ((0, 4), (1, 32)), -0.2, 0.2), 0.0, 1.0),
        "tf_color": jnp.clip(jax.random.uniform(arg_keys[1], (3, KNOTS), jnp.float32, 0.0, 1.0), 0.0, 1.0).astype(jnp.bfloat16),
        "tf_extinction": jnp.clip(jnp.exp(jax.random.uniform(arg_keys[2], (KNOTS,), jnp.float32, math.log(0.0019989014), math.log(0.049804688))), 0.0019989014, 0.049804688).astype(jnp.bfloat16),
        "brick_map": draw_brick_map(jax.random.fold_in(arg_keys[7], 71), 0),
        "view_order": draw_view_order(jax.random.fold_in(arg_keys[7], 71), 0),
        "anchors": draw_anchors(jax.random.fold_in(arg_keys[7], 71), 0),
        "rects": draw_rects(jax.random.fold_in(arg_keys[7], 71), 0),
    }


def render_brick(density, tf_table, bounds):
    position = density * float(KNOTS - 1)
    lower_knot = jnp.clip(jnp.floor(position), 0.0, float(KNOTS - 2))
    lower_weight = jnp.maximum(0.0, 1.0 - jnp.abs(position - lower_knot)).astype(jnp.bfloat16).astype(jnp.float32)
    upper_weight = jnp.maximum(0.0, 1.0 - jnp.abs(position - (lower_knot + 1.0))).astype(jnp.bfloat16).astype(jnp.float32)
    knot_index = lower_knot.astype(jnp.int32)
    table_wide = tf_table.astype(jnp.float32)
    looked_up = table_wide[:, knot_index] * lower_weight[None] + table_wide[:, knot_index + 1] * upper_weight[None]
    row_index = jnp.arange(FOOT_H, dtype=jnp.int32)[:, None]
    col_index = jnp.arange(FOOT_W, dtype=jnp.int32)[None, :]
    inside = (row_index >= bounds[0]) & (row_index < bounds[1]) & (col_index >= bounds[2]) & (col_index < bounds[3])
    extinction = jnp.where(inside[None], looked_up[3], 0.0)
    optical_depth = jnp.cumsum(extinction, axis=0)
    weights = jnp.exp(-(optical_depth - extinction)) - jnp.exp(-optical_depth)
    premult = jnp.sum(weights[None] * looked_up[:3], axis=1)
    opacity = 1.0 - jnp.exp(-optical_depth[-1])
    return jnp.concatenate([premult, opacity[None]], axis=0)


def reference(brick_field, tf_color, tf_extinction, brick_map, view_order, anchors, rects):
    tf_table = jnp.concatenate([tf_color, tf_extinction[None]], axis=0)
    fields = brick_field.reshape(BRICKS, SAMPLES, FOOT_H, FOOT_W)
    numbers = jnp.arange(BRICKS, dtype=jnp.int32)

    def accumulate(frame_image, rank_now):
        brick_id = view_order[rank_now]
        slot_now = jnp.sum(jnp.where(brick_map == brick_id, numbers, 0)).astype(jnp.int32)
        density = lax.dynamic_index_in_dim(fields, slot_now, 0, keepdims=False)
        partial_value = render_brick(density, tf_table, rects[brick_id])
        anchor = anchors[brick_id]
        placed = lax.dynamic_update_slice(jnp.zeros((4, IMG_H, IMG_W), jnp.float32), partial_value, (jnp.int32(0), anchor[0].astype(jnp.int32), anchor[1].astype(jnp.int32)))
        return frame_image + (1.0 - frame_image[3:4]) * placed, None

    frame_image, unused = lax.scan(accumulate, jnp.zeros((4, IMG_H, IMG_W), jnp.float32), numbers)
    return frame_image
```

```python
import functools

import jax
import jax.numpy as jnp
from jax import lax
from jax.experimental import pallas as pl
from jax.experimental.pallas import tpu as pltpu
from jax.sharding import PartitionSpec as P

DMA = pltpu.SemaphoreType.DMA
VMEM = pl.BlockSpec(memory_space=pltpu.VMEM)
SMEM = pl.BlockSpec(memory_space=pltpu.SMEM)
SAMPLES = 32
PLANE = 32


def as_bf16(value):
    return value.astype(jnp.bfloat16).astype(jnp.float32)


def render_kernel(
    brick_map, view_order, anchors, rects, field, color, extinct, rows_out, meta, image, table, slot_of
):
    layer = lax.axis_index("depth")
    my_slot = layer * PLANE + lax.axis_index("screen")
    brick = brick_map[my_slot]
    row0, col0 = anchors[brick, 0], anchors[brick, 1]
    first_row, end_row = rects[brick, 0], rects[brick, 1]
    first_col, end_col = rects[brick, 2], rects[brick, 3]

    def note_slot(slot, carry):
        slot_of[brick_map[slot]] = slot
        return carry

    lax.fori_loop(0, 128, note_slot, 0, unroll=8)
    base = jnp.int32(0)
    for place in range(4):
        owner = slot_of[view_order[place * PLANE]] // PLANE
        meta[96 + place] = owner
        base = jnp.where(owner == layer, place * PLANE, base)

    def note_rank(index, carry):
        now = view_order[base + index]
        meta[index] = lax.rem(slot_of[now], PLANE)
        meta[32 + index] = anchors[now, 0]
        meta[64 + index] = anchors[now, 1]
        return carry

    lax.fori_loop(0, PLANE, note_rank, 0, unroll=4)

    colors = color[...].astype(jnp.float32)
    depths = extinct[...].astype(jnp.float32)
    for which in range(4):
        line = colors[which : which + 1] if which < 3 else depths
        line = jnp.broadcast_to(line, (8, 128))
        table[which] = line
        table[4 + which] = pltpu.roll(line, 127, 1)
    lower = [table[which] for which in range(4)]
    upper = [table[4 + which] for which in range(4)]
    row_index = lax.broadcasted_iota(jnp.int32, (8, 128), 0)
    col_index = lax.broadcasted_iota(jnp.int32, (8, 128), 1)
    col_inside = (col_index >= first_col) & (col_index < end_col)
    zero = jnp.zeros((8, 128), jnp.float32)
    turn = lax.rem(col0, 128)

    def group(step, carry):
        start = pl.multiple_of(step * 8, 8)
        depth = zero
        clear = zero + 1.0
        sums = [zero, zero, zero]
        for sample in range(SAMPLES):
            position = field[0, 0, sample, pl.ds(start, 8), :] * 127.0
            knot = jnp.minimum(position.astype(jnp.int32), 126)
            part = position - knot.astype(jnp.float32)
            low_weight, up_weight = as_bf16(1.0 - part), as_bf16(part)
            value = [
                jnp.take_along_axis(lower[which], knot, axis=1) * low_weight
                + jnp.take_along_axis(upper[which], knot, axis=1) * up_weight
                for which in range(4)
            ]
            depth = depth + value[3]
            behind = jnp.exp(-depth)
            weight = clear - behind
            clear = behind
            sums = [total + weight * one for total, one in zip(sums, value)]
        row = row_index + start
        inside = col_inside & (row >= first_row) & (row < end_row)
        target = lax.rem(start + row0, 128)
        for which, total in enumerate([*sums, 1.0 - clear]):
            image[which, pl.ds(target, 8), :] = pltpu.roll(jnp.where(inside, total, 0.0), turn, 1)
        return carry

    lax.fori_loop(0, 16, group, 0)
    spill = lax.rem(row0, 8)
    for which in range(4):
        head = jnp.where(row_index < spill, image[which, 128:136, :], image[which, 0:8, :])
        image[which, 0:8, :] = head
    for which in range(4):
        rows_out[:, which] = image[which, 0:128, :].reshape(PLANE, 4, 128)


def wrap(value):
    return lax.rem(value + 8, 4)


def combine_kernel(
    meta, rows, out, parts, layer_send, layer_parts, a2a_send, a2a_recv, own_sem,
    y_send, y_recv, first_send, first_recv, second_send, second_recv, twin_send, twin_recv,
):
    layer, screen = lax.axis_index("depth"), lax.axis_index("screen")
    z, x, core = screen // 8, lax.rem(screen // 2, 4), lax.rem(screen, 2)
    chip = screen // 2
    twin = {"screen": chip * 2 + 1 - core}
    others = [(wrap(layer + step), side) for step in (1, 2, 3) for side in range(2)]

    barrier = pltpu.get_barrier_semaphore()
    for step in range(1, PLANE):
        pl.semaphore_signal(barrier, inc=1, device_id={"screen": lax.rem(screen + step, PLANE)})
    for strip, side in others:
        pl.semaphore_signal(barrier, inc=1, device_id={"depth": strip, "screen": chip * 2 + side})
    pl.semaphore_wait(barrier, PLANE - 1 + len(others))

    sends = []
    for step in range(1, PLANE):
        peer = lax.rem(screen + step, PLANE)
        copy = pltpu.make_async_remote_copy(
            rows.at[peer], parts.at[screen], a2a_send.at[step], a2a_recv.at[step], device_id={"screen": peer}
        )
        copy.start()
        sends.append(copy)
    own = pltpu.make_async_copy(rows.at[screen], parts.at[screen], own_sem)
    own.start()
    own.wait()
    for copy in sends:
        copy.wait_recv()

    sub = lax.broadcasted_iota(jnp.int32, (8, 128), 0)
    lane = lax.broadcasted_iota(jnp.int32, (8, 128), 1)
    first_half = sub < 4
    half = jnp.where(first_half, 0, 1)
    row_class = screen * 4 + lax.rem(sub, 4)
    zero = jnp.zeros((8, 128), jnp.float32)

    def strip_image(strip):
        def brick(index, state):
            clear, sums = state
            source, row0, col0 = meta[index], meta[32 + index], meta[64 + index]
            block = jnp.right_shift(row0 - row_class + 127, 7)
            column = jnp.right_shift(col0, 7) + jnp.where(lane < jnp.bitwise_and(col0, 127), 1, 0)
            key = block * 8 + column - half - 2 * strip
            pair = [parts[source, 0], parts[source, 1]]
            swapped = [pltpu.roll(one, 4, 0) for one in pair]
            comps = []
            for one, other in zip(pair, swapped):
                comps += [jnp.where(first_half, one, other), jnp.where(first_half, other, one)]
            new_clear, new_sums = [], []
            for spot in range(4):
                weight = jnp.where(key == spot * 8, clear[spot], 0.0)
                new_clear.append(clear[spot] - weight * comps[3])
                new_sums.append([sums[spot][which] + weight * comps[which] for which in range(3)])
            return new_clear, new_sums

        return lax.fori_loop(
            0, PLANE, brick, ([zero + 1.0] * 4, [[zero] * 3 for _ in range(4)]), unroll=4
        )

    y_copies = []
    for step in (1, 2, 3, 0):
        strip = wrap(layer + step)
        clear, sums = strip_image(strip)
        for spot in range(4):
            for which in range(4):
                value = sums[spot][which] if which < 3 else 1.0 - clear[spot]
                layer_send[step, spot // 2, which, spot % 2] = value
        for side in range(2):
            if step:
                copy = pltpu.make_async_remote_copy(
                    layer_send.at[step, side], layer_parts.at[layer, core],
                    y_send.at[step, side], y_recv.at[step, core],
                    device_id={"depth": strip, "screen": chip * 2 + side},
                )
                copy.start()
                y_copies.append((side, copy))
    keep = pltpu.make_async_copy(layer_send.at[0, core], layer_parts.at[layer, core], own_sem)
    keep.start()
    copy = pltpu.make_async_remote_copy(
        layer_send.at[0, 1 - core], layer_parts.at[layer, core], y_send.at[0, 0], y_recv.at[0, 0], device_id=twin
    )
    copy.start()
    keep.wait()
    copy.wait_recv()
    sends.append(copy)
    for step in (1, 2, 3):
        for side in range(2):
            arrival = pltpu.make_async_remote_copy(
                layer_send.at[step, 0], layer_parts.at[wrap(layer - step), side],
                y_send.at[step, side], y_recv.at[step, side], device_id=twin,
            )
            arrival.wait_recv()
    sends += [copy for _, copy in y_copies]

    tops, bottoms = [], []
    for side in range(2):
        for spot in range(2):
            clear = zero + 1.0
            sums = [zero] * 3
            for place in range(4):
                one = meta[96 + place]
                sums = [sums[which] + clear * layer_parts[one, side, which, spot] for which in range(3)]
                clear = clear - clear * layer_parts[one, side, 3, spot]
            (bottoms if side else tops).append([*sums, 1.0 - clear])
    for spot in range(2):
        for which in range(4):
            top, bottom = tops[spot][which], bottoms[spot][which]
            left = jnp.where(first_half, top, pltpu.roll(bottom, 4, 0))
            right = jnp.where(first_half, pltpu.roll(top, 4, 0), bottom)
            out[which, core * 2 + spot, chip, :, 0:128] = left
            out[which, core * 2 + spot, chip, :, 128:256] = right

    def spot_of(first, second):
        dz = jnp.where(core == 0, second, first)
        dx = jnp.where(core == 0, first, second)
        return wrap(z + dz) * 4 + wrap(x + dx)

    def tile(first, second):
        return out.at[:, pl.ds(2 * core, 2), spot_of(first, second)]

    def device(first, second):
        return {"screen": spot_of(first, second) * 2 + core}

    def push(region, send, recv, target):
        copy = pltpu.make_async_remote_copy(region, region, send, recv, device_id=target)
        copy.start()
        sends.append(copy)
        return copy

    twins = []

    def to_twin(first, second):
        index = len(twins)
        twins.append(push(tile(first, second), twin_send.at[index], twin_recv.at[index], twin))

    firsts = {step: push(tile(0, 0), first_send.at[step], first_recv.at[step], device(step, 0)) for step in (1, 3, 2)}
    seconds = {}

    def second_phase(gone):
        for step in (1, 3, 2):
            seconds[gone, step] = push(
                tile(-gone, 0), second_send.at[gone, step], second_recv.at[gone, step], device(0, step)
            )

    second_phase(0)
    to_twin(0, 0)
    for step in (1, 3, 2):
        firsts[step].wait_recv()
        second_phase(step)
        to_twin(-step, 0)
    for gone in (0, 1, 3, 2):
        for step in (1, 3, 2):
            seconds[gone, step].wait_recv()
            to_twin(-gone, -step)
    for copy in twins:
        copy.wait_recv()
    for copy in sends:
        copy.wait_send()


def shards(brick_field, tf_color, tf_extinction, brick_map, view_order, anchors, rects):
    rows, meta = pl.pallas_call(
        render_kernel,
        out_shape=(
            jax.ShapeDtypeStruct((PLANE, 4, 4, 128), jnp.float32),
            jax.ShapeDtypeStruct((128,), jnp.int32),
        ),
        in_specs=[SMEM] * 4 + [VMEM] * 3,
        out_specs=(VMEM, SMEM),
        scratch_shapes=[
            pltpu.VMEM((4, 136, 128), jnp.float32),
            pltpu.VMEM((8, 8, 128), jnp.float32),
            pltpu.SMEM((128,), jnp.int32),
        ],
        compiler_params=pltpu.CompilerParams(vmem_limit_bytes=32 * 2**20),
        name="render",
    )(brick_map, view_order, anchors, rects, brick_field, tf_color, tf_extinction.reshape(1, 128))
    out = pl.pallas_call(
        combine_kernel,
        out_shape=pltpu.VMEM((4, 4, 16, 8, 256), jnp.float32),
        in_specs=[SMEM, VMEM],
        out_specs=VMEM,
        scratch_shapes=[
            pltpu.VMEM((PLANE, 2, 8, 128), jnp.float32),
            pltpu.VMEM((4, 2, 4, 2, 8, 128), jnp.float32),
            pltpu.VMEM((4, 2, 4, 2, 8, 128), jnp.float32),
            DMA((PLANE,)), DMA((PLANE,)), DMA(()),
            DMA((4, 2)), DMA((4, 2)),
            DMA((4,)), DMA((4,)), DMA((4, 4)), DMA((4, 4)), DMA((16,)), DMA((16,)),
        ],
        compiler_params=pltpu.CompilerParams(
            collective_id=0, has_side_effects=True, vmem_limit_bytes=32 * 2**20
        ),
        name="combine",
    )(meta, rows.reshape(PLANE, 2, 8, 128))
    return out.reshape(4, 512, 256)


def solution(mesh):
    placed = (P("depth", "screen", None, None, None), P(), P(), P(), P(), P(), P())
    return jax.shard_map(
        shards, mesh=mesh, in_specs=placed, out_specs=P(None, None, "depth"), check_vma=False
    )
```

```python
import jax
import jax.numpy as jnp
from jax import lax
from jax.experimental import pallas as pl
from jax.experimental.pallas import tpu as pltpu
from jax.sharding import PartitionSpec as P

DMA = pltpu.SemaphoreType.DMA
HBM = pl.BlockSpec(memory_space=pltpu.HBM)
VMEM = pl.BlockSpec(memory_space=pltpu.VMEM)
SAMPLES = 32
PLANE = 32
PICK = lax.GatherDimensionNumbers(
    offset_dims=(), collapsed_slice_dims=(1,), start_index_map=(1,),
    operand_batching_dims=(0,), start_indices_batching_dims=(0,),
)


def pick(table, lanes):
    return lax.gather(table, lanes[..., None], PICK, (1, 1), mode=lax.GatherScatterMode.PROMISE_IN_BOUNDS)


def wrap(value):
    return lax.rem(value + 8, 4)


def frame_kernel(
    brick_map, view_order, anchors, rects, field, color, extinct, out,
    map_v, order_v, anchors_v, rects_v, color_v, extinct_v, map_s, notes_v, notes, field_v,
    rows, parts, layer_send, even_parts, odd_parts,
    in_sem, field_sem, a2a_send, a2a_recv,
    y_send, y_recv, first_send, first_recv, second_send, second_recv, twin_send, twin_recv,
):
    layer, screen = lax.axis_index("depth"), lax.axis_index("screen")
    z, x, core = screen // 8, lax.rem(screen // 2, 4), lax.rem(screen, 2)
    chip = screen // 2
    twin = {"screen": chip * 2 + 1 - core}
    others = [(wrap(layer + step), side) for step in (1, 2, 3) for side in range(2)]

    small = [
        pltpu.make_async_copy(source, target, in_sem.at[index])
        for index, (source, target) in enumerate([
            (brick_map, map_s), (brick_map, map_v), (view_order, order_v), (anchors, anchors_v),
            (rects, rects_v), (color, color_v), (extinct, extinct_v),
        ])
    ]
    for copy in small:
        copy.start()
    big = [
        pltpu.make_async_copy(field.at[0, 0], field_v.at[:, pl.ds(0, 128)], field_sem.at[0]),
        pltpu.make_async_copy(field.at[0, 0, :, pl.ds(0, 16)], field_v.at[:, pl.ds(128, 16)], field_sem.at[1]),
    ]
    for copy in big:
        copy.start()

    barrier = pltpu.get_barrier_semaphore()
    for step in range(1, PLANE):
        pl.semaphore_signal(barrier, inc=1, device_id={"screen": lax.rem(screen + step, PLANE)})
    for strip, side in others:
        pl.semaphore_signal(barrier, inc=1, device_id={"depth": strip, "screen": chip * 2 + side})

    sub = lax.broadcasted_iota(jnp.int32, (8, 128), 0)
    lane = lax.broadcasted_iota(jnp.int32, (8, 128), 1)
    zero = jnp.zeros((8, 128), jnp.float32)

    for copy in small:
        copy.wait()
    order = jnp.bitwise_and(jnp.broadcast_to(order_v[...], (8, 128)), 127)
    slots = jnp.zeros((8, 128), jnp.int32)
    for slot in range(128):
        slots = jnp.where(order == map_s[0, slot], slot, slots)
    bricks = jnp.bitwise_and(jnp.broadcast_to(map_v[...], (8, 128)), 127)
    lines = [slots]
    for table, count in ((anchors_v, 2), (rects_v, 4)):
        for which in range(count):
            line = jnp.broadcast_to(table[which : which + 1, :], (8, 128))
            if count == 2:
                lines.append(pick(line, order))
            lines.append(pick(line, bricks))
    for index, line in enumerate(lines):
        notes_v[index : index + 1, :] = line[0:1]
    note_copy = pltpu.make_async_copy(notes_v, notes, in_sem.at[0])
    note_copy.start()
    note_copy.wait()
    my_slot = layer * PLANE + screen
    row0, col0 = notes[2, my_slot], notes[4, my_slot]
    first_row, end_row = notes[5, my_slot], notes[6, my_slot]
    first_col, end_col = notes[7, my_slot], notes[8, my_slot]

    lower, upper = [], []
    for which in range(4):
        line = color_v[which : which + 1, :] if which < 3 else extinct_v[...]
        line = jnp.broadcast_to(line.astype(jnp.float32), (16, 128))
        lower.append(line.astype(jnp.bfloat16))
        upper.append(pltpu.roll(line, 127, 1).astype(jnp.bfloat16))
    row_index = lax.broadcasted_iota(jnp.int32, (16, 128), 0)
    col_index = lax.broadcasted_iota(jnp.int32, (16, 128), 1)
    col_inside = (col_index >= first_col) & (col_index < end_col)
    blank = jnp.zeros((16, 128), jnp.float32)
    turn = jnp.bitwise_and(col0, 127)
    for copy in big:
        copy.wait()

    def group(step, carry):
        owner0 = lax.rem(screen // 4 + 1 + step, 8) * 4
        start = jnp.bitwise_and(owner0 * 4 - row0, 127)
        depth, clear, sums = blank, blank + 1.0, [blank] * 3
        for sample in range(SAMPLES):
            position = field_v[sample, pl.ds(start, 16), :] * 127.0
            knot = jnp.floor(position)
            part = position - knot
            lanes = jnp.bitwise_and(knot.astype(jnp.int32).astype(jnp.int16), jnp.int16(127))
            low = (1.0 - part).astype(jnp.bfloat16).astype(jnp.float32)
            up = part.astype(jnp.bfloat16).astype(jnp.float32)
            below = [pick(table, lanes).astype(jnp.float32) for table in lower]
            above = [pick(table, lanes).astype(jnp.float32) for table in upper]
            depth = depth - (below[3] * low + above[3] * up)
            behind = jnp.exp(depth)
            weight = clear - behind
            clear = behind
            low, up = low * weight, up * weight
            sums = [sums[which] + (below[which] * low + above[which] * up) for which in range(3)]
        row = lax.rem(row_index + start, 128)
        inside = col_inside & (row >= first_row) & (row < end_row)
        for which, total in enumerate([*sums, 1.0 - clear]):
            total = pltpu.roll(jnp.where(inside, total, 0.0), turn, 1)
            for index in range(4):
                rows[owner0 + index, which // 2, pl.ds(which % 2 * 4, 4), :] = total[index * 4 : index * 4 + 4]

        @pl.when(step == 0)
        def _():
            pl.semaphore_wait(barrier, PLANE - 1 + len(others))

        for index in range(4):
            peer = owner0 + index

            @pl.when(peer != screen)
            def _():
                pltpu.make_async_remote_copy(
                    rows.at[peer], parts.at[screen], a2a_send.at[peer], a2a_recv.at[screen],
                    device_id={"screen": peer},
                ).start()

            @pl.when(peer == screen)
            def _():
                pltpu.make_async_copy(rows.at[peer], parts.at[screen], a2a_recv.at[screen]).start()
        return carry

    lax.fori_loop(0, 8, group, 0)

    places = [jnp.bitwise_and(jnp.right_shift(notes[0, place * PLANE], 5), 3) for place in range(4)]
    base = jnp.int32(0)
    for place in range(4):
        base = jnp.where(places[place] == layer, place * PLANE, base)
    first_half = sub < 4
    half = jnp.where(first_half, 0, 1)
    row_class = screen * 4 + lax.rem(sub, 4)

    def arrive(source, carry):
        pltpu.make_async_copy(parts.at[source], parts.at[source], a2a_recv.at[source]).wait()
        return carry

    lax.fori_loop(0, PLANE, arrive, 0)

    y_copies = {}
    layer_parts = [even_parts, odd_parts]
    for part in range(2):
        def brick(index, state):
            clear, sums = state
            source = jnp.bitwise_and(notes[0, base + index], PLANE - 1)
            row_at, col_at = notes[1, base + index], notes[3, base + index]
            block = jnp.right_shift(row_at - row_class + 127, 7)
            column = jnp.right_shift(col_at, 7) + jnp.where(lane < jnp.bitwise_and(col_at, 127), 1, 0)
            key = block * 8 + column - half
            pair = [parts[source, 0], parts[source, 1]]
            swapped = [pltpu.roll(one, 4, 0) for one in pair]
            comps = []
            for one, other in zip(pair, swapped):
                comps += [jnp.where(first_half, one, other), jnp.where(first_half, other, one)]
            new_clear, new_sums = [], []
            for spot in range(8):
                weight = jnp.where(key == (spot % 2 * 2 + part) * 8 + spot // 2 * 2, clear[spot], 0.0)
                new_clear.append(clear[spot] - weight * comps[3])
                new_sums.append([sums[spot][which] + weight * comps[which] for which in range(3)])
            return new_clear, new_sums

        clear, sums = lax.fori_loop(
            0, PLANE, brick, ([zero + 1.0] * 8, [[zero] * 3 for _ in range(8)]), unroll=4
        )
        for spot in range(8):
            for which in range(4):
                value = sums[spot][which] if which < 3 else 1.0 - clear[spot]
                layer_send[part, spot // 2, spot % 2, which] = value
        for step in (1, 2, 3):
            strip = wrap(layer + step)
            for side in range(2):
                copy = pltpu.make_async_remote_copy(
                    layer_send.at[part, strip, side], layer_parts[part].at[layer, core],
                    y_send.at[part, step, side], y_recv.at[part, step, core],
                    device_id={"depth": strip, "screen": chip * 2 + side},
                )
                copy.start()
                y_copies[part, step, side] = copy
        keep = pltpu.make_async_copy(
            layer_send.at[part, layer, core], layer_parts[part].at[layer, core], y_recv.at[part, 0, 0]
        )
        keep.start()
        copy = pltpu.make_async_remote_copy(
            layer_send.at[part, layer, 1 - core], layer_parts[part].at[layer, core],
            y_send.at[part, 0, 1], y_recv.at[part, 0, 1], device_id=twin,
        )
        copy.start()
        y_copies[part, 0, 1] = copy
        y_copies[part, 0, 0] = keep

    sends = [copy for key, copy in y_copies.items() if key[1:] != (0, 0)]

    def spot_of(first, second):
        dz = jnp.where(core == 0, second, first)
        dx = jnp.where(core == 0, first, second)
        return wrap(z + dz) * 4 + wrap(x + dx)

    def device(first, second):
        return {"screen": spot_of(first, second) * 2 + core}

    def push(region, send, recv, target):
        copy = pltpu.make_async_remote_copy(region, region, send, recv, device_id=target)
        copy.start()
        sends.append(copy)
        return copy

    def tile(part, first, second):
        return out.at[:, 2 * core + part, spot_of(first, second)]

    twins, firsts, seconds = [], {}, {}

    def to_twin(part, first, second):
        index = len(twins)
        twins.append(push(tile(part, first, second), twin_send.at[index], twin_recv.at[index], twin))

    def second_phase(part, gone):
        for step in (1, 3, 2):
            seconds[part, gone, step] = push(
                tile(part, -gone, 0), second_send.at[part, gone, step], second_recv.at[part, gone, step],
                device(0, step),
            )

    for part in range(2):
        y_copies[part, 0, 0].wait()
        y_copies[part, 0, 1].wait_recv()
        for step in (1, 2, 3):
            for side in range(2):
                arrived = layer_parts[part].at[wrap(layer - step), side]
                pltpu.make_async_copy(arrived, arrived, y_recv.at[part, step, side]).wait()
        halves = []
        for side in range(2):
            clear, sums = zero + 1.0, [zero] * 3
            for place in range(4):
                one = places[place]
                sums = [sums[which] + clear * layer_parts[part][one, side, which] for which in range(3)]
                clear = clear - clear * layer_parts[part][one, side, 3]
            halves.append([*sums, 1.0 - clear])
        for which in range(4):
            top, bottom = halves[0][which], halves[1][which]
            out[which, core * 2 + part, chip, :, 0:128] = jnp.where(first_half, top, pltpu.roll(bottom, 4, 0))
            out[which, core * 2 + part, chip, :, 128:256] = jnp.where(first_half, pltpu.roll(top, 4, 0), bottom)
        for step in (1, 3, 2):
            firsts[part, step] = push(
                tile(part, 0, 0), first_send.at[part, step], first_recv.at[part, step], device(step, 0)
            )
        second_phase(part, 0)
        to_twin(part, 0, 0)

    for part in range(2):
        for step in (1, 3, 2):
            firsts[part, step].wait_recv()
            second_phase(part, step)
            to_twin(part, -step, 0)
    for part in range(2):
        for gone in (0, 1, 3, 2):
            for step in (1, 3, 2):
                seconds[part, gone, step].wait_recv()
                to_twin(part, -gone, -step)
    for copy in twins:
        copy.wait_recv()
    for copy in sends:
        copy.wait_send()

    def left(peer, carry):
        @pl.when(peer != screen)
        def _():
            pltpu.make_async_copy(rows.at[peer], rows.at[peer], a2a_send.at[peer]).wait()
        return carry

    lax.fori_loop(0, PLANE, left, 0)


def shards(brick_field, tf_color, tf_extinction, brick_map, view_order, anchors, rects):
    out = pl.pallas_call(
        frame_kernel,
        out_shape=pltpu.VMEM((4, 4, 16, 8, 256), jnp.float32),
        in_specs=[HBM] * 7,
        out_specs=VMEM,
        scratch_shapes=[
            pltpu.VMEM((1, 128), jnp.int32), pltpu.VMEM((1, 128), jnp.int32),
            pltpu.VMEM((2, 128), jnp.int32), pltpu.VMEM((4, 128), jnp.int32),
            pltpu.VMEM((3, 128), jnp.bfloat16), pltpu.VMEM((1, 128), jnp.bfloat16),
            pltpu.SMEM((1, 128), jnp.int32), pltpu.VMEM((16, 128), jnp.int32), pltpu.SMEM((16, 128), jnp.int32),
            pltpu.VMEM((SAMPLES, 144, 128), jnp.float32),
            pltpu.VMEM((PLANE, 2, 8, 128), jnp.float32),
            pltpu.VMEM((PLANE, 2, 8, 128), jnp.float32),
            pltpu.VMEM((2, 4, 2, 4, 8, 128), jnp.float32),
            pltpu.VMEM((4, 2, 4, 8, 128), jnp.float32),
            pltpu.VMEM((4, 2, 4, 8, 128), jnp.float32),
            DMA((7,)), DMA((2,)), DMA((PLANE,)), DMA((PLANE,)),
            DMA((2, 4, 2)), DMA((2, 4, 2)),
            DMA((2, 4)), DMA((2, 4)), DMA((2, 4, 4)), DMA((2, 4, 4)), DMA((32,)), DMA((32,)),
        ],
        compiler_params=pltpu.CompilerParams(
            collective_id=0, has_side_effects=True, vmem_limit_bytes=56 * 2**20
        ),
        name="frame",
    )(
        brick_map.reshape(1, 128), view_order.reshape(1, 128), anchors.T, rects.T,
        brick_field, tf_color, tf_extinction.reshape(1, 128),
    )
    return out.reshape(4, 512, 256)


def solution(mesh):
    placed = (P("depth", "screen", None, None, None), P(), P(), P(), P(), P(), P())
    return jax.shard_map(
        shards, mesh=mesh, in_specs=placed, out_specs=P(None, None, "depth"), check_vma=False
    )
```

```python
import jax
import jax.numpy as jnp
from jax import lax
from jax.experimental import pallas as pl
from jax.experimental.pallas import tpu as pltpu
from jax.sharding import PartitionSpec as P

DMA = pltpu.SemaphoreType.DMA
HBM = pl.BlockSpec(memory_space=pltpu.HBM)
VMEM = pl.BlockSpec(memory_space=pltpu.VMEM)
SAMPLES = 32
PLANE = 32
PICK = lax.GatherDimensionNumbers(
    offset_dims=(), collapsed_slice_dims=(1,), start_index_map=(1,),
    operand_batching_dims=(0,), start_indices_batching_dims=(0,),
)


def pick(table, lanes):
    return lax.gather(table, lanes[..., None], PICK, (1, 1), mode=lax.GatherScatterMode.PROMISE_IN_BOUNDS)


def wrap(value):
    return lax.rem(value + 8, 4)


def frame_kernel(
    brick_map, view_order, anchors, rects, field, color, extinct, out,
    map_v, order_v, anchors_v, color_v, extinct_v, map_s, anchors_s, rects_s, notes_v, notes, field_v,
    rows, first_parts, second_parts, layer_send, first_layers, second_layers,
    in_sem, field_sem, a2a_send, a2a_recv, y_send, y_recv,
    tile_send, first_recv, second_recv, twin_send, twin_recv,
):
    layer, screen = lax.axis_index("depth"), lax.axis_index("screen")
    z, x, core = screen // 8, lax.rem(screen // 2, 4), lax.rem(screen, 2)
    chip, pair, member = screen // 2, screen // 4, lax.rem(screen, 4)
    twin = {"screen": chip * 2 + 1 - core}
    parts, layers = [first_parts, second_parts], [first_layers, second_layers]

    small = [
        pltpu.make_async_copy(source, target, in_sem.at[index])
        for index, (source, target) in enumerate([
            (brick_map, map_s), (anchors, anchors_s), (rects, rects_s), (color, color_v), (extinct, extinct_v),
            (brick_map, map_v), (view_order, order_v), (anchors, anchors_v),
        ])
    ]
    big = [
        pltpu.make_async_copy(field.at[0, 0], field_v.at[:, pl.ds(0, 128)], field_sem.at[0]),
        pltpu.make_async_copy(field.at[0, 0, :, pl.ds(0, 16)], field_v.at[:, pl.ds(128, 16)], field_sem.at[1]),
    ]
    for copy in small + big:
        copy.start()

    barrier = pltpu.get_barrier_semaphore()

    def greet(step, carry):
        pl.semaphore_signal(barrier, inc=1, device_id={"screen": lax.rem(screen + step, PLANE)})
        return carry

    lax.fori_loop(1, PLANE, greet, 0)
    for step in (1, 2, 3):
        for index in range(4):
            pl.semaphore_signal(barrier, inc=1, device_id={"depth": wrap(layer + step), "screen": pair * 4 + index})
    greetings = PLANE - 1 + 12

    sub = lax.broadcasted_iota(jnp.int32, (8, 128), 0)
    lane = lax.broadcasted_iota(jnp.int32, (8, 128), 1)
    zero = jnp.zeros((8, 128), jnp.float32)

    for copy in small:
        copy.wait()
    order = jnp.bitwise_and(jnp.broadcast_to(order_v[...], (8, 128)), 127)
    slots = jnp.zeros((8, 128), jnp.int32)
    for slot in range(128):
        slots = jnp.where(order == map_s[0, slot], slot, slots)
    lines = [slots] + [pick(jnp.broadcast_to(anchors_v[which : which + 1, :], (8, 128)), order) for which in range(2)]
    for index, line in enumerate(lines):
        notes_v[index : index + 1, :] = line[0:1]
    note_copy = pltpu.make_async_copy(notes_v, notes, in_sem.at[0])
    note_copy.start()
    brick_id = jnp.bitwise_and(map_s[0, layer * PLANE + screen], 127)
    row0, col0 = anchors_s[0, brick_id], anchors_s[1, brick_id]
    first_row, end_row = rects_s[0, brick_id], rects_s[1, brick_id]
    first_col, end_col = rects_s[2, brick_id], rects_s[3, brick_id]

    lower, upper = [], []
    for which in range(4):
        line = color_v[which : which + 1, :] if which < 3 else extinct_v[...]
        line = jnp.broadcast_to(line.astype(jnp.float32), (16, 128))
        lower.append(line.astype(jnp.bfloat16))
        upper.append(pltpu.roll(line, 127, 1).astype(jnp.bfloat16))
    row_index = lax.broadcasted_iota(jnp.int32, (16, 128), 0)
    col_index = lax.broadcasted_iota(jnp.int32, (16, 128), 1)
    col_inside = (col_index >= first_col) & (col_index < end_col)
    blank = jnp.zeros((16, 128), jnp.float32)
    turn = jnp.bitwise_and(col0, 127)
    for copy in big:
        copy.wait()

    def render(stage, step):
        owner0 = lax.rem(screen // 8 + 1 + step, 4) * 8
        start = jnp.bitwise_and(stage * 64 + owner0 * 2 - row0, 127)
        depth, clear, sums = blank, blank + 1.0, [blank] * 3
        for sample in range(SAMPLES):
            position = field_v[sample, pl.ds(start, 16), :] * 127.0
            knot = jnp.floor(position)
            part = position - knot
            lanes = jnp.bitwise_and(knot.astype(jnp.int32).astype(jnp.int16), jnp.int16(127))
            low = (1.0 - part).astype(jnp.bfloat16).astype(jnp.float32)
            up = part.astype(jnp.bfloat16).astype(jnp.float32)
            below = [pick(table, lanes).astype(jnp.float32) for table in lower]
            above = [pick(table, lanes).astype(jnp.float32) for table in upper]
            depth = depth - (below[3] * low + above[3] * up)
            behind = jnp.exp(depth)
            weight = clear - behind
            clear = behind
            low, up = low * weight, up * weight
            sums = [sums[which] + (below[which] * low + above[which] * up) for which in range(3)]
        row = jnp.bitwise_and(row_index + start, 127)
        inside = col_inside & (row >= first_row) & (row < end_row)
        for which, total in enumerate([*sums, 1.0 - clear]):
            total = pltpu.roll(jnp.where(inside, total, 0.0), turn, 1)
            for index in range(8):
                rows[stage, owner0 + index, which * 2 : which * 2 + 2, :] = total[index * 2 : index * 2 + 2]

        if stage == 0:
            @pl.when(step == 0)
            def _():
                pl.semaphore_wait(barrier, greetings)

        def send(peer):
            pltpu.make_async_remote_copy(
                rows.at[stage, peer], parts[stage].at[screen], a2a_send.at[stage], a2a_recv.at[stage],
                device_id={"screen": peer},
            ).start()

        for index in range(1, 8):
            send(owner0 + lax.rem(screen + index, 8))

        @pl.when(step < 3)
        def _():
            send(owner0 + lax.rem(screen, 8))

        @pl.when(step == 3)
        def _():
            pltpu.make_async_copy(rows.at[stage, screen], parts[stage].at[screen], a2a_recv.at[stage]).start()

    for stage in range(2):
        def group(step, carry, stage=stage):
            render(stage, step)
            return carry

        lax.fori_loop(0, 4, group, 0)

    note_copy.wait()
    places = [jnp.bitwise_and(jnp.right_shift(notes[0, place * PLANE], 5), 3) for place in range(4)]
    base = jnp.int32(0)
    for place in range(4):
        base = jnp.where(places[place] == layer, place * PLANE, base)
    odd_row = jnp.bitwise_and(sub, 1) == 1
    spot_col = jnp.right_shift(sub, 1)

    def all_of(ref, sem):
        pltpu.make_async_copy(ref, ref, sem).wait()

    def composite(stage):
        row_class = stage * 64 + screen * 2 + jnp.bitwise_and(sub, 1)
        all_of(parts[stage], a2a_recv.at[stage])

        def brick(index, state):
            clear, sums = state
            source = jnp.bitwise_and(notes[0, base + index], PLANE - 1)
            row_at, col_at = notes[1, base + index], notes[2, base + index]
            block = jnp.right_shift(row_at - row_class + 127, 7)
            column = jnp.right_shift(col_at, 7) + jnp.where(lane < jnp.bitwise_and(col_at, 127), 1, 0)
            key = block * 8 + column - spot_col
            comps = []
            for which in range(4):
                even, odd = [
                    jnp.broadcast_to(parts[stage][source, pl.ds(which * 2 + side, 1), :], (8, 128)) for side in range(2)
                ]
                comps.append(jnp.where(odd_row, odd, even))
            new_clear, new_sums = [], []
            for spot in range(8):
                weight = jnp.where(key == spot * 4, clear[spot], 0.0)
                new_clear.append(clear[spot] - weight * comps[3])
                new_sums.append([sums[spot][which] + weight * comps[which] for which in range(3)])
            return new_clear, new_sums

        clear, sums = lax.fori_loop(
            0, PLANE, brick, ([zero + 1.0] * 8, [[zero] * 3 for _ in range(8)]), unroll=4
        )
        for spot in range(8):
            for which in range(4):
                value = sums[spot][which] if which < 3 else 1.0 - clear[spot]
                for side in range(2):
                    layer_send[stage, spot % 2 * 2 + side, spot // 2, which] = value[side * 4 : side * 4 + 4]
        for step in (2, 1, 3, 0):
            strip = wrap(layer + step)
            for turned in range(4):
                block = lax.rem(member + turned, 4)
                source, target = layer_send.at[stage, strip, block], layers[stage].at[layer, :, member]
                if step or turned:
                    pltpu.make_async_remote_copy(
                        source, target, y_send.at[stage], y_recv.at[stage],
                        device_id={"depth": strip, "screen": pair * 4 + block},
                    ).start()
                else:
                    pltpu.make_async_copy(source, target, y_recv.at[stage]).start()

    def spot_of(first, second):
        dz = jnp.where(core == 0, second, first)
        dx = jnp.where(core == 0, first, second)
        return wrap(z + dz) * 4 + wrap(x + dx)

    def tile(stage, first, second):
        spot = spot_of(first, second)
        return out.at[:, lax.rem(spot, 2) * 2 + core, stage * 8 + spot // 2]

    def push(stage, first, second, recv, target, send):
        region = tile(stage, first, second)
        copy = pltpu.make_async_remote_copy(region, region, send, recv, device_id=target)
        copy.start()
        return copy

    firsts, seconds = {}, {}

    def to_twin(stage, first, second):
        push(stage, first, second, twin_recv, twin, twin_send)

    def second_phase(stage, gone):
        for step in (1, 3, 2):
            seconds[stage, gone, step] = push(
                stage, -gone, 0, second_recv.at[stage, gone, step],
                {"screen": spot_of(0, step) * 2 + core}, tile_send.at[stage],
            )

    def finish(stage):
        all_of(layers[stage], y_recv.at[stage])
        for source in range(4):
            clear, sums = jnp.ones((4, 128), jnp.float32), [jnp.zeros((4, 128), jnp.float32)] * 3
            for place in range(4):
                one = places[place]
                sums = [sums[which] + clear * layers[stage][one, which, source] for which in range(3)]
                clear = clear - clear * layers[stage][one, 3, source]
            for which, value in enumerate([*sums, 1.0 - clear]):
                for side in range(2):
                    out[which, member, stage * 8 + pair, source * 2 : source * 2 + 2, side * 128 : side * 128 + 128] = (
                        value[side * 2 : side * 2 + 2]
                    )
        for step in (1, 3, 2):
            firsts[stage, step] = push(
                stage, 0, 0, first_recv.at[stage, step], {"screen": spot_of(step, 0) * 2 + core}, tile_send.at[stage]
            )
        second_phase(stage, 0)
        to_twin(stage, 0, 0)

    def forward(stage):
        for step in (1, 3, 2):
            firsts[stage, step].wait_recv()
            second_phase(stage, step)
            to_twin(stage, -step, 0)

    def collect(stage):
        for gone in (0, 1, 3, 2):
            for step in (1, 3, 2):
                seconds[stage, gone, step].wait_recv()
                to_twin(stage, -gone, -step)

    composite(0)
    composite(1)
    finish(0)
    finish(1)
    forward(0)
    forward(1)
    collect(0)
    collect(1)
    all_of(out.at[:, pl.ds(0, 2)], twin_recv)
    all_of(out.at[:, pl.ds(0, 2)], twin_send)
    for stage in range(2):
        all_of(out.at[:, 0, pl.ds(0, 15)], tile_send.at[stage])
        all_of(rows.at[stage, pl.ds(0, PLANE - 1)], a2a_send.at[stage])
        all_of(layers[stage].at[pl.ds(0, 3)], y_send.at[stage])
        all_of(layers[stage].at[0, pl.ds(0, 3)], y_send.at[stage])


def shards(brick_field, tf_color, tf_extinction, brick_map, view_order, anchors, rects):
    out = pl.pallas_call(
        frame_kernel,
        out_shape=pltpu.VMEM((4, 4, 16, 8, 256), jnp.float32),
        in_specs=[HBM] * 7,
        out_specs=VMEM,
        scratch_shapes=[
            pltpu.VMEM((1, 128), jnp.int32), pltpu.VMEM((1, 128), jnp.int32), pltpu.VMEM((2, 128), jnp.int32),
            pltpu.VMEM((3, 128), jnp.bfloat16), pltpu.VMEM((1, 128), jnp.bfloat16),
            pltpu.SMEM((1, 128), jnp.int32), pltpu.SMEM((2, 128), jnp.int32), pltpu.SMEM((4, 128), jnp.int32),
            pltpu.VMEM((8, 128), jnp.int32), pltpu.SMEM((8, 128), jnp.int32),
            pltpu.VMEM((SAMPLES, 144, 128), jnp.float32),
            pltpu.VMEM((2, PLANE, 8, 128), jnp.float32),
            pltpu.VMEM((PLANE, 8, 128), jnp.float32),
            pltpu.VMEM((PLANE, 8, 128), jnp.float32),
            pltpu.VMEM((2, 4, 4, 4, 4, 128), jnp.float32),
            pltpu.VMEM((4, 4, 4, 4, 128), jnp.float32),
            pltpu.VMEM((4, 4, 4, 4, 128), jnp.float32),
            DMA((8,)), DMA((2,)), DMA((2,)), DMA((2,)), DMA((2,)), DMA((2,)),
            DMA((2,)), DMA((2, 4)), DMA((2, 4, 4)), DMA(()), DMA(()),
        ],
        compiler_params=pltpu.CompilerParams(
            collective_id=0, has_side_effects=True, vmem_limit_bytes=56 * 2**20
        ),
        name="frame",
    )(
        brick_map.reshape(1, 128), view_order.reshape(1, 128), anchors.T, rects.T,
        brick_field, tf_color, tf_extinction.reshape(1, 128),
    )
    return out.reshape(4, 512, 256)


def solution(mesh):
    placed = (P("depth", "screen", None, None, None), P(), P(), P(), P(), P(), P())
    return jax.shard_map(
        shards, mesh=mesh, in_specs=placed, out_specs=P(None, None, "depth"), check_vma=False
    )
```

```python
import jax
import jax.numpy as jnp
from jax import lax
from jax.experimental import pallas as pl
from jax.experimental.pallas import tpu as pltpu
from jax.sharding import PartitionSpec as P

DMA = pltpu.SemaphoreType.DMA
HBM = pl.BlockSpec(memory_space=pltpu.HBM)
VMEM = pl.BlockSpec(memory_space=pltpu.VMEM)
SAMPLES = 32
PLANE = 32
STAGES = 4
PICK = lax.GatherDimensionNumbers(
    offset_dims=(), collapsed_slice_dims=(1,), start_index_map=(1,),
    operand_batching_dims=(0,), start_indices_batching_dims=(0,),
)


def pick(table, lanes):
    return lax.gather(table, lanes[..., None], PICK, (1, 1), mode=lax.GatherScatterMode.PROMISE_IN_BOUNDS)


def wrap(value):
    return lax.rem(value + 8, 4)


def frame_kernel(
    brick_map, view_order, anchors, rects, field, color, extinct, out,
    map_v, order_v, anchors_v, color_v, extinct_v, map_s, anchors_s, rects_s, notes_v, notes, field_v,
    rows, parts, layer_send, layers,
    in_sem, field_sem, a2a_send, a2a_recv, y_send, y_recv,
    tile_send, first_recv, second_recv, twin_send, twin_recv,
):
    layer, screen = lax.axis_index("depth"), lax.axis_index("screen")
    z, x, core = screen // 8, lax.rem(screen // 2, 4), lax.rem(screen, 2)
    chip = screen // 2
    twin = {"screen": chip * 2 + 1 - core}

    small = [
        pltpu.make_async_copy(source, target, in_sem.at[index])
        for index, (source, target) in enumerate([
            (brick_map, map_s), (anchors, anchors_s), (rects, rects_s), (color, color_v), (extinct, extinct_v),
            (brick_map, map_v), (view_order, order_v), (anchors, anchors_v),
        ])
    ]
    big = [
        pltpu.make_async_copy(field.at[0, 0], field_v.at[:, pl.ds(0, 128)], field_sem.at[0]),
        pltpu.make_async_copy(field.at[0, 0, :, pl.ds(0, 16)], field_v.at[:, pl.ds(128, 16)], field_sem.at[1]),
    ]
    for copy in small + big:
        copy.start()

    barrier = pltpu.get_barrier_semaphore()

    def greet(step, carry):
        pl.semaphore_signal(barrier, inc=1, device_id={"screen": lax.rem(screen + step, PLANE)})
        return carry

    lax.fori_loop(1, PLANE, greet, 0)
    for step in (1, 2, 3):
        for index in range(2):
            pl.semaphore_signal(barrier, inc=1, device_id={"depth": wrap(layer + step), "screen": chip * 2 + index})
    greetings = PLANE - 1 + 6

    sub = lax.broadcasted_iota(jnp.int32, (8, 128), 0)
    lane = lax.broadcasted_iota(jnp.int32, (8, 128), 1)
    zero = jnp.zeros((8, 128), jnp.float32)

    for copy in small:
        copy.wait()
    order = jnp.bitwise_and(jnp.broadcast_to(order_v[...], (8, 128)), 127)
    slots = jnp.zeros((8, 128), jnp.int32)
    for slot in range(128):
        slots = jnp.where(order == map_s[0, slot], slot, slots)
    lines = [slots] + [pick(jnp.broadcast_to(anchors_v[which : which + 1, :], (8, 128)), order) for which in range(2)]
    for index, line in enumerate(lines):
        notes_v[index : index + 1, :] = line[0:1]
    note_copy = pltpu.make_async_copy(notes_v, notes, in_sem.at[0])
    note_copy.start()
    brick_id = jnp.bitwise_and(map_s[0, layer * PLANE + screen], 127)
    row0, col0 = anchors_s[0, brick_id], anchors_s[1, brick_id]
    first_row, end_row = rects_s[0, brick_id], rects_s[1, brick_id]
    first_col, end_col = rects_s[2, brick_id], rects_s[3, brick_id]

    lower, upper = [], []
    for which in range(4):
        line = color_v[which : which + 1, :] if which < 3 else extinct_v[...]
        line = jnp.broadcast_to(line.astype(jnp.float32), (16, 128))
        lower.append(line.astype(jnp.bfloat16))
        upper.append(pltpu.roll(line, 127, 1).astype(jnp.bfloat16))
    row_index = lax.broadcasted_iota(jnp.int32, (16, 128), 0)
    col_index = lax.broadcasted_iota(jnp.int32, (16, 128), 1)
    col_inside = (col_index >= first_col) & (col_index < end_col)
    blank = jnp.zeros((16, 128), jnp.float32)
    turn = jnp.bitwise_and(col0, 127)
    for copy in big:
        copy.wait()

    def render(stage, near):
        owner0 = (z // 2 if near else 1 - z // 2) * 16
        start = jnp.bitwise_and(stage * PLANE + owner0 - row0, 127)
        depth, clear, sums = blank, blank + 1.0, [blank] * 3
        for sample in range(SAMPLES):
            position = field_v[sample, pl.ds(start, 16), :] * 127.0
            knot = jnp.floor(position)
            part = position - knot
            lanes = jnp.bitwise_and(knot.astype(jnp.int32).astype(jnp.int16), jnp.int16(127))
            low = (1.0 - part).astype(jnp.bfloat16).astype(jnp.float32)
            up = part.astype(jnp.bfloat16).astype(jnp.float32)
            below = [pick(table, lanes).astype(jnp.float32) for table in lower]
            above = [pick(table, lanes).astype(jnp.float32) for table in upper]
            depth = depth - (below[3] * low + above[3] * up)
            behind = jnp.exp(depth)
            weight = clear - behind
            clear = behind
            low, up = low * weight, up * weight
            sums = [sums[which] + (below[which] * low + above[which] * up) for which in range(3)]
        row = jnp.bitwise_and(row_index + start, 127)
        inside = col_inside & (row >= first_row) & (row < end_row)
        for which, total in enumerate([*sums, 1.0 - clear]):
            total = pltpu.roll(jnp.where(inside, total, 0.0), turn, 1)
            for index in range(16):
                rows[stage, owner0 + index, which : which + 1, :] = total[index : index + 1]

    def send(stage, near):
        owner0 = (z // 2 if near else 1 - z // 2) * 16
        for index in range(16):
            peer = owner0 + lax.rem(screen + index, 16)
            if near and index == 0:
                pltpu.make_async_copy(rows.at[stage, screen], parts[stage].at[screen], a2a_recv.at[stage]).start()
            else:
                pltpu.make_async_remote_copy(
                    rows.at[stage, peer], parts[stage].at[screen], a2a_send.at[stage], a2a_recv.at[stage],
                    device_id={"screen": peer},
                ).start()

    turns = [(0, False), (1, False), (0, True), (2, False), (1, True), (3, False), (2, True), (3, True)]
    for index, now in enumerate(turns):
        if index == 1:
            pl.semaphore_wait(barrier, greetings)
        if index:
            send(*turns[index - 1])
        render(*now)
    send(*turns[-1])

    note_copy.wait()
    places = [jnp.bitwise_and(jnp.right_shift(notes[0, place * PLANE], 5), 3) for place in range(4)]
    base = jnp.int32(0)
    for place in range(4):
        base = jnp.where(places[place] == layer, place * PLANE, base)
    def all_of(ref, sem):
        pltpu.make_async_copy(ref, ref, sem).wait()

    def composite(stage):
        row_class = stage * PLANE + screen
        all_of(parts[stage], a2a_recv.at[stage])

        def brick(index, state):
            clear, sums = state
            source = jnp.bitwise_and(notes[0, base + index], PLANE - 1)
            row_at, col_at = notes[1, base + index], notes[2, base + index]
            block = jnp.right_shift(row_at - row_class + 127, 7)
            column = jnp.right_shift(col_at, 7) + jnp.where(lane < jnp.bitwise_and(col_at, 127), 1, 0)
            key = block * 8 + column - sub
            comps = [
                jnp.broadcast_to(parts[stage][source, pl.ds(which, 1), :], (8, 128)) for which in range(4)
            ]
            new_clear, new_sums = [], []
            for spot in range(4):
                weight = jnp.where(key == spot * 8, clear[spot], 0.0)
                new_clear.append(clear[spot] - weight * comps[3])
                new_sums.append([sums[spot][which] + weight * comps[which] for which in range(3)])
            return new_clear, new_sums

        clear, sums = lax.fori_loop(
            0, PLANE, brick, ([zero + 1.0] * 4, [[zero] * 3 for _ in range(4)]), unroll=4
        )
        for spot in range(4):
            for which in range(4):
                value = sums[spot][which] if which < 3 else 1.0 - clear[spot]
                for strip in range(4):
                    layer_send[stage, strip, spot, which] = value[strip * 2 : strip * 2 + 2]
        for step in (2, 1, 3, 0):
            strip = wrap(layer + step)
            for turned in range(2):
                side = lax.rem(core + turned, 2)
                source, target = layer_send.at[stage, strip, pl.ds(side * 2, 2)], layers[stage].at[layer, core]
                if step or turned:
                    pltpu.make_async_remote_copy(
                        source, target, y_send.at[stage], y_recv.at[stage],
                        device_id={"depth": strip, "screen": chip * 2 + side},
                    ).start()
                else:
                    pltpu.make_async_copy(source, target, y_recv.at[stage]).start()

    def spot_of(first, second):
        dz = jnp.where(core == 0, second, first)
        dx = jnp.where(core == 0, first, second)
        return wrap(z + dz) * 4 + wrap(x + dx)

    def tile(stage, first, second):
        spot = spot_of(first, second)
        lines = pl.ds(pl.multiple_of(lax.rem(spot, 4) * 2, 2), 2)
        return out.at[:, pl.ds(core * 2, 2), stage * 4 + spot // 4, lines]

    def push(stage, first, second, recv, target, send):
        region = tile(stage, first, second)
        copy = pltpu.make_async_remote_copy(region, region, send, recv, device_id=target)
        copy.start()
        return copy

    def landed(sem):
        piece = out.at[:, pl.ds(0, 2), 0, pl.ds(0, 2)]
        pltpu.make_async_copy(piece, piece, sem).wait()

    def to_twin(stage, gone):
        region = out.at[:, pl.ds(core * 2, 2), stage * 4 + wrap(z - gone)]
        pltpu.make_async_remote_copy(region, region, twin_send, twin_recv, device_id=twin).start()

    def group(gone, step):
        return jnp.where(core == 0, step, gone), jnp.where(core == 0, gone, step)

    def second_phase(stage, gone):
        for step in (1, 3, 2):
            push(
                stage, -gone, 0, second_recv.at[(stage, *group(gone, step))], {"screen": spot_of(0, step) * 2 + core},
                tile_send,
            )

    def finish(stage):
        all_of(layers[stage], y_recv.at[stage])
        values = []
        for spot in range(2):
            sides = []
            for source in range(2):
                clear, sums = jnp.ones((2, 128), jnp.float32), [jnp.zeros((2, 128), jnp.float32)] * 3
                for place in range(4):
                    one = places[place]
                    sums = [sums[which] + clear * layers[stage][one, source, spot, which] for which in range(3)]
                    clear = clear - clear * layers[stage][one, source, spot, 3]
                sides.append([*sums, 1.0 - clear])
            values.append([
                [jnp.concatenate([one[which][side : side + 1] for one in sides], axis=0) for side in range(2)]
                for which in range(4)
            ])
        for turned in range(4):
            @pl.when(lax.rem(chip, 4) == turned)
            def _():
                for spot in range(2):
                    for which in range(4):
                        for side in range(2):
                            out[
                                which, core * 2 + spot, stage * 4 + z, turned * 2 : turned * 2 + 2,
                                side * 128 : side * 128 + 128,
                            ] = values[spot][which][side]

        for step in (1, 3, 2):
            push(stage, 0, 0, first_recv.at[stage, step], {"screen": spot_of(step, 0) * 2 + core}, tile_send)
        second_phase(stage, 0)

    def forward(stage, carry):
        for step in (1, 3, 2):
            landed(first_recv.at[stage, step])
            second_phase(stage, step)
        return carry

    def collect(stage, carry):
        for gone in (0, 1, 3, 2):
            if gone:
                for place in (1, 3, 2):
                    landed(second_recv.at[stage, gone, place])

            @pl.when(core == (0 if gone else 1))
            def _():
                for place in (0,) if gone else (1, 3, 2):
                    landed(second_recv.at[stage, gone, place])

            to_twin(stage, gone)
        return carry

    for work in (composite, finish):
        for stage in range(STAGES):
            work(stage)
    lax.fori_loop(0, STAGES, forward, 0)
    lax.fori_loop(0, STAGES, collect, 0)
    all_of(out.at[:, pl.ds(0, 2)], twin_recv)
    all_of(out.at[:, pl.ds(0, 2)], twin_send)
    all_of(out.at[:, pl.ds(0, 2), pl.ds(0, 15)], tile_send)
    for stage in range(STAGES):
        all_of(rows.at[stage, pl.ds(0, PLANE - 1)], a2a_send.at[stage])
        all_of(layers[stage].at[pl.ds(0, 3)], y_send.at[stage])
        all_of(layers[stage].at[0, 0], y_send.at[stage])


def shards(brick_field, tf_color, tf_extinction, brick_map, view_order, anchors, rects):
    out = pl.pallas_call(
        frame_kernel,
        out_shape=pltpu.VMEM((4, 4, 16, 8, 256), jnp.float32),
        in_specs=[HBM] * 7,
        out_specs=VMEM,
        scratch_shapes=[
            pltpu.VMEM((1, 128), jnp.int32), pltpu.VMEM((1, 128), jnp.int32), pltpu.VMEM((2, 128), jnp.int32),
            pltpu.VMEM((3, 128), jnp.bfloat16), pltpu.VMEM((1, 128), jnp.bfloat16),
            pltpu.SMEM((1, 128), jnp.int32), pltpu.SMEM((2, 128), jnp.int32), pltpu.SMEM((4, 128), jnp.int32),
            pltpu.VMEM((8, 128), jnp.int32), pltpu.SMEM((8, 128), jnp.int32),
            pltpu.VMEM((SAMPLES, 144, 128), jnp.float32),
            pltpu.VMEM((STAGES, PLANE, 4, 128), jnp.float32),
            tuple(pltpu.VMEM((PLANE, 4, 128), jnp.float32) for _ in range(STAGES)),
            pltpu.VMEM((STAGES, 4, 4, 4, 2, 128), jnp.float32),
            tuple(pltpu.VMEM((4, 2, 2, 4, 2, 128), jnp.float32) for _ in range(STAGES)),
            DMA((8,)), DMA((2,)), DMA((STAGES,)), DMA((STAGES,)), DMA((STAGES,)), DMA((STAGES,)),
            DMA(()), DMA((STAGES, 4)), DMA((STAGES, 4, 4)), DMA(()), DMA(()),
        ],
        compiler_params=pltpu.CompilerParams(
            collective_id=0, has_side_effects=True, vmem_limit_bytes=56 * 2**20
        ),
        name="frame",
    )(
        brick_map.reshape(1, 128), view_order.reshape(1, 128), anchors.T, rects.T,
        brick_field, tf_color, tf_extinction.reshape(1, 128),
    )
    return out.reshape(4, 512, 256)


def solution(mesh):
    placed = (P("depth", "screen", None, None, None), P(), P(), P(), P(), P(), P())
    return jax.shard_map(
        shards, mesh=mesh, in_specs=placed, out_specs=P(None, None, "depth"), check_vma=False
    )
```

```python
import jax
import jax.numpy as jnp
from jax import lax
from jax.experimental import pallas as pl
from jax.experimental.pallas import tpu as pltpu
from jax.sharding import PartitionSpec as P

DMA = pltpu.SemaphoreType.DMA
HBM = pl.BlockSpec(memory_space=pltpu.HBM)
VMEM = pl.BlockSpec(memory_space=pltpu.VMEM)
SAMPLES = 32
CHUNK = 8
PLANE = 32
STAGES = 4
PICK = lax.GatherDimensionNumbers(
    offset_dims=(), collapsed_slice_dims=(1,), start_index_map=(1,),
    operand_batching_dims=(0,), start_indices_batching_dims=(0,),
)


def pick(table, lanes):
    return lax.gather(table, lanes[..., None], PICK, (1, 1), mode=lax.GatherScatterMode.PROMISE_IN_BOUNDS)


def wrap(value):
    return lax.rem(value + 8, 4)


def frame_kernel(
    brick_map, view_order, anchors, rects, field, color, extinct, out,
    map_v, order_v, anchors_v, color_v, extinct_v, map_s, anchors_s, rects_s, notes_v, notes, field_v,
    rows, parts, layer_send, layers,
    in_sem, field_sem, a2a_send, a2a_recv, y_send, y_recv,
    tile_send, first_recv, second_recv, twin_send, twin_recv,
):
    layer, screen = lax.axis_index("depth"), lax.axis_index("screen")
    z, x, core = screen // 8, lax.rem(screen // 2, 4), lax.rem(screen, 2)
    chip = screen // 2
    twin = {"screen": chip * 2 + 1 - core}

    small = [
        pltpu.make_async_copy(source, target, in_sem.at[index])
        for index, (source, target) in enumerate([
            (brick_map, map_s), (anchors, anchors_s), (rects, rects_s), (color, color_v), (extinct, extinct_v),
            (brick_map, map_v), (view_order, order_v), (anchors, anchors_v),
        ])
    ]
    big = [
        pltpu.make_async_copy(
            field.at[0, 0, pl.ds(chunk * CHUNK, CHUNK), pl.ds(0, lines)],
            field_v[chunk].at[:, pl.ds(at, lines)], field_sem.at[chunk, part],
        )
        for chunk in range(SAMPLES // CHUNK) for part, (at, lines) in enumerate(((0, 128), (128, 16)))
    ]
    for copy in small + big:
        copy.start()

    barrier = pltpu.get_barrier_semaphore()

    def greet(step, carry):
        pl.semaphore_signal(barrier, inc=1, device_id={"screen": lax.rem(screen + step, PLANE)})
        return carry

    lax.fori_loop(1, PLANE, greet, 0)
    for step in (1, 2, 3):
        for index in range(2):
            pl.semaphore_signal(barrier, inc=1, device_id={"depth": wrap(layer + step), "screen": chip * 2 + index})
    greetings = PLANE - 1 + 6

    sub = lax.broadcasted_iota(jnp.int32, (8, 128), 0)
    lane = lax.broadcasted_iota(jnp.int32, (8, 128), 1)
    zero = jnp.zeros((8, 128), jnp.float32)

    for copy in small:
        copy.wait()
    order = jnp.bitwise_and(jnp.broadcast_to(order_v[...], (8, 128)), 127)
    slots = jnp.zeros((8, 128), jnp.int32)
    for slot in range(128):
        slots = jnp.where(order == map_s[0, slot], slot, slots)
    lines = [slots] + [pick(jnp.broadcast_to(anchors_v[which : which + 1, :], (8, 128)), order) for which in range(2)]
    for index, line in enumerate(lines):
        notes_v[index : index + 1, :] = line[0:1]
    note_copy = pltpu.make_async_copy(notes_v, notes, in_sem.at[0])
    note_copy.start()
    brick_id = jnp.bitwise_and(map_s[0, layer * PLANE + screen], 127)
    row0, col0 = anchors_s[0, brick_id], anchors_s[1, brick_id]
    first_row, end_row = rects_s[0, brick_id], rects_s[1, brick_id]
    first_col, end_col = rects_s[2, brick_id], rects_s[3, brick_id]

    lower, upper = [], []
    for which in range(4):
        line = color_v[which : which + 1, :] if which < 3 else extinct_v[...]
        line = jnp.broadcast_to(line.astype(jnp.float32), (16, 128))
        lower.append(line.astype(jnp.bfloat16))
        upper.append(pltpu.roll(line, 127, 1).astype(jnp.bfloat16))
    row_index = lax.broadcasted_iota(jnp.int32, (16, 128), 0)
    col_index = lax.broadcasted_iota(jnp.int32, (16, 128), 1)
    col_inside = (col_index >= first_col) & (col_index < end_col)
    blank = jnp.zeros((16, 128), jnp.float32)
    turn = jnp.bitwise_and(col0, 127)
    def render(stage, near, waits):
        owner0 = (z // 2 if near else 1 - z // 2) * 16
        start = jnp.bitwise_and(stage * PLANE + owner0 - row0, 127)
        depth, clear, sums = blank, blank + 1.0, [blank] * 3
        for sample in range(SAMPLES):
            if sample % CHUNK == 0:
                for copy in waits[sample // CHUNK * 2 : sample // CHUNK * 2 + 2]:
                    copy.wait()
            position = field_v[sample // CHUNK][sample % CHUNK, pl.ds(start, 16), :] * 127.0
            knot = jnp.floor(position)
            part = position - knot
            lanes = jnp.bitwise_and(knot.astype(jnp.int32).astype(jnp.int16), jnp.int16(127))
            low = (1.0 - part).astype(jnp.bfloat16).astype(jnp.float32)
            up = part.astype(jnp.bfloat16).astype(jnp.float32)
            below = [pick(table, lanes).astype(jnp.float32) for table in lower]
            above = [pick(table, lanes).astype(jnp.float32) for table in upper]
            depth = depth - (below[3] * low + above[3] * up)
            behind = jnp.exp(depth)
            weight = clear - behind
            clear = behind
            low, up = low * weight, up * weight
            sums = [sums[which] + (below[which] * low + above[which] * up) for which in range(3)]
        row = jnp.bitwise_and(row_index + start, 127)
        inside = col_inside & (row >= first_row) & (row < end_row)
        for which, total in enumerate([*sums, 1.0 - clear]):
            total = pltpu.roll(jnp.where(inside, total, 0.0), turn, 1)
            rows[stage, which, pl.ds(pl.multiple_of(owner0, 16), 16), :] = total

    def send(stage, near):
        owner0 = (z // 2 if near else 1 - z // 2) * 16
        for index in range(16):
            peer = owner0 + lax.rem(screen + index, 16)
            if near and index == 0:
                pltpu.make_async_copy(rows.at[stage, :, pl.ds(screen, 1)], parts[stage].at[screen], a2a_recv.at[stage]).start()
            else:
                pltpu.make_async_remote_copy(
                    rows.at[stage, :, pl.ds(peer, 1)], parts[stage].at[screen], a2a_send.at[stage], a2a_recv.at[stage],
                    device_id={"screen": peer},
                ).start()

    turns = [(0, False), (1, False), (0, True), (2, False), (1, True), (3, False), (2, True), (3, True)]
    for index, now in enumerate(turns):
        if index == 3:
            pl.semaphore_wait(barrier, greetings)
            for earlier in turns[:index - 1]:
                send(*earlier)
        if index >= 3:
            send(*turns[index - 1])
        render(*now, big if index == 0 else [])
    send(*turns[-1])

    note_copy.wait()
    places = [jnp.bitwise_and(jnp.right_shift(notes[0, place * PLANE], 5), 3) for place in range(4)]
    base = jnp.int32(0)
    for place in range(4):
        base = jnp.where(places[place] == layer, place * PLANE, base)
    def all_of(ref, sem):
        pltpu.make_async_copy(ref, ref, sem).wait()

    def composite(stage):
        row_class = stage * PLANE + screen
        all_of(parts[stage], a2a_recv.at[stage])

        def brick(index, state):
            clear, sums = state
            source = jnp.bitwise_and(notes[0, base + index], PLANE - 1)
            row_at, col_at = notes[1, base + index], notes[2, base + index]
            block = jnp.right_shift(row_at - row_class + 127, 7)
            column = jnp.right_shift(col_at, 7) + jnp.where(lane < jnp.bitwise_and(col_at, 127), 1, 0)
            key = block * 8 + column - sub
            comps = [
                jnp.broadcast_to(parts[stage][source, which], (8, 128)) for which in range(4)
            ]
            new_clear, new_sums = [], []
            for spot in range(4):
                weight = jnp.where(key == spot * 8, clear[spot], 0.0)
                new_clear.append(clear[spot] - weight * comps[3])
                new_sums.append([sums[spot][which] + weight * comps[which] for which in range(3)])
            return new_clear, new_sums

        clear, sums = lax.fori_loop(
            0, PLANE, brick, ([zero + 1.0] * 4, [[zero] * 3 for _ in range(4)]), unroll=4
        )
        for spot in range(4):
            for which in range(4):
                value = sums[spot][which] if which < 3 else 1.0 - clear[spot]
                for strip in range(4):
                    layer_send[stage, strip, spot, which] = value[strip * 2 : strip * 2 + 2]
        for step in (2, 1, 3, 0):
            strip = wrap(layer + step)
            for turned in range(2):
                side = lax.rem(core + turned, 2)
                source, target = layer_send.at[stage, strip, pl.ds(side * 2, 2)], layers[stage].at[layer, core]
                if step or turned:
                    pltpu.make_async_remote_copy(
                        source, target, y_send.at[stage], y_recv.at[stage],
                        device_id={"depth": strip, "screen": chip * 2 + side},
                    ).start()
                else:
                    pltpu.make_async_copy(source, target, y_recv.at[stage]).start()

    def spot_of(first, second):
        dz = jnp.where(core == 0, second, first)
        dx = jnp.where(core == 0, first, second)
        return wrap(z + dz) * 4 + wrap(x + dx)

    def tile(stage, first, second):
        spot = spot_of(first, second)
        lines = pl.ds(pl.multiple_of(lax.rem(spot, 4) * 2, 2), 2)
        return out.at[:, pl.ds(core * 2, 2), stage * 4 + spot // 4, lines]

    def push(stage, first, second, recv, target, send):
        region = tile(stage, first, second)
        copy = pltpu.make_async_remote_copy(region, region, send, recv, device_id=target)
        copy.start()
        return copy

    def landed(sem):
        piece = out.at[:, pl.ds(0, 2), 0, pl.ds(0, 2)]
        pltpu.make_async_copy(piece, piece, sem).wait()

    def to_twin(stage, gone):
        region = out.at[:, pl.ds(core * 2, 2), stage * 4 + wrap(z - gone)]
        pltpu.make_async_remote_copy(region, region, twin_send, twin_recv, device_id=twin).start()

    def second_phase(stage, gone):
        for step in (1, 3, 2):
            push(
                stage, -gone, 0, second_recv.at[stage, gone, step], {"screen": spot_of(0, step) * 2 + core}, tile_send
            )

    def finish(stage):
        all_of(layers[stage], y_recv.at[stage])
        values = []
        for spot in range(2):
            sides = []
            for source in range(2):
                clear, sums = jnp.ones((2, 128), jnp.float32), [jnp.zeros((2, 128), jnp.float32)] * 3
                for place in range(4):
                    one = places[place]
                    sums = [sums[which] + clear * layers[stage][one, source, spot, which] for which in range(3)]
                    clear = clear - clear * layers[stage][one, source, spot, 3]
                sides.append([*sums, 1.0 - clear])
            values.append([
                [jnp.concatenate([one[which][side : side + 1] for one in sides], axis=0) for side in range(2)]
                for which in range(4)
            ])
        for turned in range(4):
            @pl.when(lax.rem(chip, 4) == turned)
            def _():
                for spot in range(2):
                    for which in range(4):
                        for side in range(2):
                            out[
                                which, core * 2 + spot, stage * 4 + z, turned * 2 : turned * 2 + 2,
                                side * 128 : side * 128 + 128,
                            ] = values[spot][which][side]

        for step in (1, 3, 2):
            push(stage, 0, 0, first_recv.at[stage, step], {"screen": spot_of(step, 0) * 2 + core}, tile_send)
        second_phase(stage, 0)

    def forward(stage):
        for step in (1, 3, 2):
            landed(first_recv.at[stage, step])
            second_phase(stage, step)

    def collect(stage):
        @pl.when(core == 0)
        def _():
            to_twin(stage, 0)
            for step in (1, 3, 2):
                for gone in (0, 1, 3, 2):
                    landed(second_recv.at[stage, gone, step])
                to_twin(stage, step)

        @pl.when(core == 1)
        def _():
            for gone in (0, 1, 3, 2):
                for step in (1, 3, 2):
                    landed(second_recv.at[stage, gone, step])
                to_twin(stage, gone)

    for work in (composite, finish, forward, collect):
        for stage in range(STAGES):
            work(stage)
    all_of(out.at[:, pl.ds(0, 2)], twin_recv)
    all_of(out.at[:, pl.ds(0, 2)], twin_send)
    all_of(out.at[:, pl.ds(0, 2), pl.ds(0, 15)], tile_send)
    for stage in range(STAGES):
        all_of(rows.at[stage, :, pl.ds(0, PLANE - 1)], a2a_send.at[stage])
        all_of(layers[stage].at[pl.ds(0, 3)], y_send.at[stage])
        all_of(layers[stage].at[0, 0], y_send.at[stage])


def shards(brick_field, tf_color, tf_extinction, brick_map, view_order, anchors, rects):
    out = pl.pallas_call(
        frame_kernel,
        out_shape=pltpu.VMEM((4, 4, 16, 8, 256), jnp.float32),
        in_specs=[HBM] * 7,
        out_specs=VMEM,
        scratch_shapes=[
            pltpu.VMEM((1, 128), jnp.int32), pltpu.VMEM((1, 128), jnp.int32), pltpu.VMEM((2, 128), jnp.int32),
            pltpu.VMEM((3, 128), jnp.bfloat16), pltpu.VMEM((1, 128), jnp.bfloat16),
            pltpu.SMEM((1, 128), jnp.int32), pltpu.SMEM((2, 128), jnp.int32), pltpu.SMEM((4, 128), jnp.int32),
            pltpu.VMEM((8, 128), jnp.int32), pltpu.SMEM((8, 128), jnp.int32),
            tuple(pltpu.VMEM((CHUNK, 144, 128), jnp.float32) for _ in range(SAMPLES // CHUNK)),
            pltpu.VMEM((STAGES, 4, PLANE, 128), jnp.float32),
            tuple(pltpu.VMEM((PLANE, 4, 1, 128), jnp.float32) for _ in range(STAGES)),
            pltpu.VMEM((STAGES, 4, 4, 4, 2, 128), jnp.float32),
            tuple(pltpu.VMEM((4, 2, 2, 4, 2, 128), jnp.float32) for _ in range(STAGES)),
            DMA((8,)), DMA((SAMPLES // CHUNK, 2)), DMA((STAGES,)), DMA((STAGES,)), DMA((STAGES,)), DMA((STAGES,)),
            DMA(()), DMA((STAGES, 4)), DMA((STAGES, 4, 4)), DMA(()), DMA(()),
        ],
        compiler_params=pltpu.CompilerParams(
            collective_id=0, has_side_effects=True, vmem_limit_bytes=56 * 2**20
        ),
        name="frame",
    )(
        brick_map.reshape(1, 128), view_order.reshape(1, 128), anchors.T, rects.T,
        brick_field, tf_color, tf_extinction.reshape(1, 128),
    )
    return out.reshape(4, 512, 256)


def solution(mesh):
    placed = (P("depth", "screen", None, None, None), P(), P(), P(), P(), P(), P())
    return jax.shard_map(
        shards, mesh=mesh, in_specs=placed, out_specs=P(None, None, "depth"), check_vma=False
    )
```

```python
import jax
import jax.numpy as jnp
from jax import lax
from jax.experimental import pallas as pl
from jax.experimental.pallas import tpu as pltpu
from jax.sharding import PartitionSpec as P

DMA = pltpu.SemaphoreType.DMA
HBM = pl.BlockSpec(memory_space=pltpu.HBM)
VMEM = pl.BlockSpec(memory_space=pltpu.VMEM)
SAMPLES = 32
CHUNK = SAMPLES
PLANE = 32
STAGES = 4
PICK = lax.GatherDimensionNumbers(
    offset_dims=(), collapsed_slice_dims=(1,), start_index_map=(1,),
    operand_batching_dims=(0,), start_indices_batching_dims=(0,),
)


def pick(table, lanes):
    return lax.gather(table, lanes[..., None], PICK, (1, 1), mode=lax.GatherScatterMode.PROMISE_IN_BOUNDS)


def wrap(value):
    return lax.rem(value + 8, 4)


def frame_kernel(
    brick_map, view_order, anchors, rects, field, color, extinct, out,
    map_v, order_v, anchors_v, color_v, extinct_v, map_s, anchors_s, rects_s, notes_v, notes, field_v,
    rows, parts, layer_send, layers,
    in_sem, field_sem, a2a_send, a2a_recv, y_send, y_recv,
    tile_send, first_recv, second_recv, twin_send, twin_recv,
):
    layer, screen = lax.axis_index("depth"), lax.axis_index("screen")
    z, x, core = screen // 8, lax.rem(screen // 2, 4), lax.rem(screen, 2)
    chip = screen // 2
    twin = {"screen": chip * 2 + 1 - core}

    small = [
        pltpu.make_async_copy(source, target, in_sem.at[index])
        for index, (source, target) in enumerate([
            (brick_map, map_s), (anchors, anchors_s), (rects, rects_s), (color, color_v), (extinct, extinct_v),
            (brick_map, map_v), (view_order, order_v), (anchors, anchors_v),
        ])
    ]
    big = [
        pltpu.make_async_copy(
            field.at[0, 0, pl.ds(chunk * CHUNK, CHUNK), pl.ds(0, lines)],
            field_v[chunk].at[:, pl.ds(at, lines)], field_sem.at[chunk, part],
        )
        for chunk in range(SAMPLES // CHUNK) for part, (at, lines) in enumerate(((0, 128), (128, 16)))
    ]
    for copy in small + big:
        copy.start()

    barrier = pltpu.get_barrier_semaphore()

    def greet(step, carry):
        pl.semaphore_signal(barrier, inc=1, device_id={"screen": lax.rem(screen + step, PLANE)})
        return carry

    lax.fori_loop(1, PLANE, greet, 0)
    for step in (1, 2, 3):
        for index in range(2):
            pl.semaphore_signal(barrier, inc=1, device_id={"depth": wrap(layer + step), "screen": chip * 2 + index})
    greetings = PLANE - 1 + 6

    sub = lax.broadcasted_iota(jnp.int32, (8, 128), 0)
    lane = lax.broadcasted_iota(jnp.int32, (8, 128), 1)
    zero = jnp.zeros((8, 128), jnp.float32)

    for copy in small:
        copy.wait()
    order = jnp.bitwise_and(jnp.broadcast_to(order_v[...], (8, 128)), 127)
    slots = jnp.zeros((8, 128), jnp.int32)
    for slot in range(128):
        slots = jnp.where(order == map_s[0, slot], slot, slots)
    lines = [slots] + [pick(jnp.broadcast_to(anchors_v[which : which + 1, :], (8, 128)), order) for which in range(2)]
    for index, line in enumerate(lines):
        notes_v[index : index + 1, :] = line[0:1]
    note_copy = pltpu.make_async_copy(notes_v, notes, in_sem.at[0])
    note_copy.start()
    brick_id = jnp.bitwise_and(map_s[0, layer * PLANE + screen], 127)
    row0, col0 = anchors_s[0, brick_id], anchors_s[1, brick_id]
    first_row, end_row = rects_s[0, brick_id], rects_s[1, brick_id]
    first_col, end_col = rects_s[2, brick_id], rects_s[3, brick_id]

    lower, upper = [], []
    for which in range(4):
        line = color_v[which : which + 1, :] if which < 3 else extinct_v[...]
        line = jnp.broadcast_to(line.astype(jnp.float32), (16, 128))
        lower.append(line.astype(jnp.bfloat16))
        upper.append(pltpu.roll(line, 127, 1).astype(jnp.bfloat16))
    row_index = lax.broadcasted_iota(jnp.int32, (16, 128), 0)
    col_index = lax.broadcasted_iota(jnp.int32, (16, 128), 1)
    col_inside = (col_index >= first_col) & (col_index < end_col)
    blank = jnp.zeros((16, 128), jnp.float32)
    turn = jnp.bitwise_and(col0, 127)
    def render(stage, near, waits):
        owner0 = (z // 2 if near else 1 - z // 2) * 16
        start = jnp.bitwise_and(stage * PLANE + owner0 - row0, 127)
        depth, clear, sums = blank, blank + 1.0, [blank] * 3
        for sample in range(SAMPLES):
            if sample % CHUNK == 0:
                for copy in waits[sample // CHUNK * 2 : sample // CHUNK * 2 + 2]:
                    copy.wait()
            position = field_v[sample // CHUNK][sample % CHUNK, pl.ds(start, 16), :] * 127.0
            knot = jnp.floor(position)
            part = position - knot
            lanes = jnp.bitwise_and(knot.astype(jnp.int32).astype(jnp.int16), jnp.int16(127))
            low = (1.0 - part).astype(jnp.bfloat16).astype(jnp.float32)
            up = part.astype(jnp.bfloat16).astype(jnp.float32)
            below = [pick(table, lanes).astype(jnp.float32) for table in lower]
            above = [pick(table, lanes).astype(jnp.float32) for table in upper]
            depth = depth - (below[3] * low + above[3] * up)
            behind = jnp.exp(depth)
            weight = clear - behind
            clear = behind
            low, up = low * weight, up * weight
            sums = [sums[which] + (below[which] * low + above[which] * up) for which in range(3)]
        row = jnp.bitwise_and(row_index + start, 127)
        inside = col_inside & (row >= first_row) & (row < end_row)
        for which, total in enumerate([*sums, 1.0 - clear]):
            total = pltpu.roll(jnp.where(inside, total, 0.0), turn, 1)
            rows[stage, which, pl.ds(pl.multiple_of(owner0, 16), 16), :] = total

    def send(stage, near):
        owner0 = (z // 2 if near else 1 - z // 2) * 16
        for index in range(16):
            peer = owner0 + lax.rem(screen + index, 16)
            if near and index == 0:
                pltpu.make_async_copy(rows.at[stage, :, pl.ds(screen, 1)], parts[stage].at[screen], a2a_recv.at[stage]).start()
            else:
                pltpu.make_async_remote_copy(
                    rows.at[stage, :, pl.ds(peer, 1)], parts[stage].at[screen], a2a_send.at[stage], a2a_recv.at[stage],
                    device_id={"screen": peer},
                ).start()

    turns = [(0, False), (1, False), (0, True), (2, False), (1, True), (3, False), (2, True), (3, True)]
    for index, now in enumerate(turns):
        if index == 3:
            pl.semaphore_wait(barrier, greetings)
            for earlier in turns[:index - 1]:
                send(*earlier)
        if index >= 3:
            send(*turns[index - 1])
        render(*now, big if index == 0 else [])
    send(*turns[-1])

    note_copy.wait()
    places = [jnp.bitwise_and(jnp.right_shift(notes[0, place * PLANE], 5), 3) for place in range(4)]
    base = jnp.int32(0)
    for place in range(4):
        base = jnp.where(places[place] == layer, place * PLANE, base)
    def all_of(ref, sem):
        pltpu.make_async_copy(ref, ref, sem).wait()

    def composite(stage):
        row_class = stage * PLANE + screen
        all_of(parts[stage], a2a_recv.at[stage])

        def brick(index, state):
            clear, sums = state
            source = jnp.bitwise_and(notes[0, base + index], PLANE - 1)
            row_at, col_at = notes[1, base + index], notes[2, base + index]
            block = jnp.right_shift(row_at - row_class + 127, 7)
            column = jnp.right_shift(col_at, 7) + jnp.where(lane < jnp.bitwise_and(col_at, 127), 1, 0)
            key = block * 8 + column - sub
            comps = [
                jnp.broadcast_to(parts[stage][source, which], (8, 128)) for which in range(4)
            ]
            new_clear, new_sums = [], []
            for spot in range(4):
                weight = jnp.where(key == spot * 8, clear[spot], 0.0)
                new_clear.append(clear[spot] - weight * comps[3])
                new_sums.append([sums[spot][which] + weight * comps[which] for which in range(3)])
            return new_clear, new_sums

        clear, sums = lax.fori_loop(
            0, PLANE, brick, ([zero + 1.0] * 4, [[zero] * 3 for _ in range(4)]), unroll=4
        )
        for spot in range(4):
            for which in range(4):
                value = sums[spot][which] if which < 3 else 1.0 - clear[spot]
                for strip in range(4):
                    layer_send[stage, strip, spot, which] = value[strip * 2 : strip * 2 + 2]
        for step in (2, 1, 3, 0):
            strip = wrap(layer + step)
            for turned in range(2):
                side = lax.rem(core + turned, 2)
                source, target = layer_send.at[stage, strip, pl.ds(side * 2, 2)], layers[stage].at[layer, core]
                if step or turned:
                    pltpu.make_async_remote_copy(
                        source, target, y_send.at[stage], y_recv.at[stage],
                        device_id={"depth": strip, "screen": chip * 2 + side},
                    ).start()
                else:
                    pltpu.make_async_copy(source, target, y_recv.at[stage]).start()

    def spot_of(first, second):
        dz = jnp.where(core == 0, second, first)
        dx = jnp.where(core == 0, first, second)
        return wrap(z + dz) * 4 + wrap(x + dx)

    def tile(stage, first, second):
        spot = spot_of(first, second)
        lines = pl.ds(pl.multiple_of(lax.rem(spot, 4) * 2, 2), 2)
        return out.at[:, pl.ds(core * 2, 2), stage * 4 + spot // 4, lines]

    def push(stage, first, second, recv, target, send):
        region = tile(stage, first, second)
        copy = pltpu.make_async_remote_copy(region, region, send, recv, device_id=target)
        copy.start()
        return copy

    def landed(sem):
        piece = out.at[:, pl.ds(0, 2), 0, pl.ds(0, 2)]
        pltpu.make_async_copy(piece, piece, sem).wait()

    def to_twin(stage, gone):
        region = out.at[:, pl.ds(core * 2, 2), stage * 4 + wrap(z - gone)]
        pltpu.make_async_remote_copy(region, region, twin_send, twin_recv, device_id=twin).start()

    def second_phase(stage, gone):
        for step in (1, 3, 2):
            push(
                stage, -gone, 0, second_recv.at[stage, gone, step], {"screen": spot_of(0, step) * 2 + core}, tile_send
            )

    def finish(stage):
        all_of(layers[stage], y_recv.at[stage])
        values = []
        for spot in range(2):
            sides = []
            for source in range(2):
                clear, sums = jnp.ones((2, 128), jnp.float32), [jnp.zeros((2, 128), jnp.float32)] * 3
                for place in range(4):
                    one = places[place]
                    sums = [sums[which] + clear * layers[stage][one, source, spot, which] for which in range(3)]
                    clear = clear - clear * layers[stage][one, source, spot, 3]
                sides.append([*sums, 1.0 - clear])
            values.append([
                [jnp.concatenate([one[which][side : side + 1] for one in sides], axis=0) for side in range(2)]
                for which in range(4)
            ])
        for turned in range(4):
            @pl.when(lax.rem(chip, 4) == turned)
            def _():
                for spot in range(2):
                    for which in range(4):
                        for side in range(2):
                            out[
                                which, core * 2 + spot, stage * 4 + z, turned * 2 : turned * 2 + 2,
                                side * 128 : side * 128 + 128,
                            ] = values[spot][which][side]

        for step in (1, 3, 2):
            push(stage, 0, 0, first_recv.at[stage, step], {"screen": spot_of(step, 0) * 2 + core}, tile_send)
        second_phase(stage, 0)

    def forward(stage):
        for step in (1, 3, 2):
            landed(first_recv.at[stage, step])
            second_phase(stage, step)

    def collect(stage):
        @pl.when(core == 0)
        def _():
            to_twin(stage, 0)
            for step in (1, 3, 2):
                for gone in (0, 1, 3, 2):
                    landed(second_recv.at[stage, gone, step])
                to_twin(stage, step)

        @pl.when(core == 1)
        def _():
            for gone in (0, 1, 3, 2):
                for step in (1, 3, 2):
                    landed(second_recv.at[stage, gone, step])
                to_twin(stage, gone)

    for work in (composite, finish, forward, collect):
        for stage in range(STAGES):
            work(stage)
    all_of(out.at[:, pl.ds(0, 2)], twin_recv)
    all_of(out.at[:, pl.ds(0, 2)], twin_send)
    all_of(out.at[:, pl.ds(0, 2), pl.ds(0, 15)], tile_send)
    for stage in range(STAGES):
        all_of(rows.at[stage, :, pl.ds(0, PLANE - 1)], a2a_send.at[stage])
        all_of(layers[stage].at[pl.ds(0, 3)], y_send.at[stage])
        all_of(layers[stage].at[0, 0], y_send.at[stage])


def shards(brick_field, tf_color, tf_extinction, brick_map, view_order, anchors, rects):
    out = pl.pallas_call(
        frame_kernel,
        out_shape=pltpu.VMEM((4, 4, 16, 8, 256), jnp.float32),
        in_specs=[HBM] * 7,
        out_specs=VMEM,
        scratch_shapes=[
            pltpu.VMEM((1, 128), jnp.int32), pltpu.VMEM((1, 128), jnp.int32), pltpu.VMEM((2, 128), jnp.int32),
            pltpu.VMEM((3, 128), jnp.bfloat16), pltpu.VMEM((1, 128), jnp.bfloat16),
            pltpu.SMEM((1, 128), jnp.int32), pltpu.SMEM((2, 128), jnp.int32), pltpu.SMEM((4, 128), jnp.int32),
            pltpu.VMEM((8, 128), jnp.int32), pltpu.SMEM((8, 128), jnp.int32),
            tuple(pltpu.VMEM((CHUNK, 144, 128), jnp.float32) for _ in range(SAMPLES // CHUNK)),
            pltpu.VMEM((STAGES, 4, PLANE, 128), jnp.float32),
            tuple(pltpu.VMEM((PLANE, 4, 1, 128), jnp.float32) for _ in range(STAGES)),
            pltpu.VMEM((STAGES, 4, 4, 4, 2, 128), jnp.float32),
            tuple(pltpu.VMEM((4, 2, 2, 4, 2, 128), jnp.float32) for _ in range(STAGES)),
            DMA((8,)), DMA((SAMPLES // CHUNK, 2)), DMA((STAGES,)), DMA((STAGES,)), DMA((STAGES,)), DMA((STAGES,)),
            DMA(()), DMA((STAGES, 4)), DMA((STAGES, 4, 4)), DMA(()), DMA(()),
        ],
        compiler_params=pltpu.CompilerParams(
            collective_id=0, has_side_effects=True, vmem_limit_bytes=56 * 2**20
        ),
        name="frame",
    )(
        brick_map.reshape(1, 128), view_order.reshape(1, 128), anchors.T, rects.T,
        brick_field, tf_color, tf_extinction.reshape(1, 128),
    )
    return out.reshape(4, 512, 256)


def solution(mesh):
    placed = (P("depth", "screen", None, None, None), P(), P(), P(), P(), P(), P())
    return jax.shard_map(
        shards, mesh=mesh, in_specs=placed, out_specs=P(None, None, "depth"), check_vma=False
    )
```

```python
import jax
import jax.numpy as jnp
from jax import lax
from jax.experimental import pallas as pl
from jax.experimental.pallas import tpu as pltpu
from jax.sharding import PartitionSpec as P

DMA = pltpu.SemaphoreType.DMA
HBM = pl.BlockSpec(memory_space=pltpu.HBM)
VMEM = pl.BlockSpec(memory_space=pltpu.VMEM)
SAMPLES = 32
CHUNK = SAMPLES
PLANE = 32
STAGES = 4
PICK = lax.GatherDimensionNumbers(
    offset_dims=(), collapsed_slice_dims=(1,), start_index_map=(1,),
    operand_batching_dims=(0,), start_indices_batching_dims=(0,),
)


def pick(table, lanes):
    return lax.gather(table, lanes[..., None], PICK, (1, 1), mode=lax.GatherScatterMode.PROMISE_IN_BOUNDS)


def wrap(value):
    return lax.rem(value + 8, 4)


def frame_kernel(
    brick_map, view_order, anchors, rects, field, color, extinct, out,
    map_v, order_v, anchors_v, color_v, extinct_v, map_s, anchors_s, rects_s, notes_v, notes, field_v,
    rows, parts, layer_send, layers,
    in_sem, field_sem, a2a_send, a2a_recv, y_send, y_recv,
    tile_send, first_recv, second_recv, twin_send, twin_recv,
):
    layer, screen = lax.axis_index("depth"), lax.axis_index("screen")
    z, x, core = screen // 8, lax.rem(screen // 2, 4), lax.rem(screen, 2)
    chip = screen // 2
    twin = {"screen": chip * 2 + 1 - core}

    small = [
        pltpu.make_async_copy(source, target, in_sem.at[index])
        for index, (source, target) in enumerate([
            (brick_map, map_s), (anchors, anchors_s), (rects, rects_s), (color, color_v), (extinct, extinct_v),
            (brick_map, map_v), (view_order, order_v), (anchors, anchors_v),
        ])
    ]
    big = [
        pltpu.make_async_copy(
            field.at[0, 0, pl.ds(chunk * CHUNK, CHUNK), pl.ds(0, lines)],
            field_v[chunk].at[:, pl.ds(at, lines)], field_sem.at[chunk, part],
        )
        for chunk in range(SAMPLES // CHUNK) for part, (at, lines) in enumerate(((0, 128), (128, 16)))
    ]
    for copy in small + big:
        copy.start()

    barrier = pltpu.get_barrier_semaphore()

    def greet(step, carry):
        pl.semaphore_signal(barrier, inc=1, device_id={"screen": lax.rem(screen + step, PLANE)})
        return carry

    lax.fori_loop(1, PLANE, greet, 0)
    for step in (1, 2, 3):
        for index in range(2):
            pl.semaphore_signal(barrier, inc=1, device_id={"depth": wrap(layer + step), "screen": chip * 2 + index})
    greetings = PLANE - 1 + 6

    sub = lax.broadcasted_iota(jnp.int32, (8, 128), 0)
    lane = lax.broadcasted_iota(jnp.int32, (8, 128), 1)
    zero = jnp.zeros((8, 128), jnp.float32)

    for copy in small:
        copy.wait()
    order = jnp.bitwise_and(jnp.broadcast_to(order_v[...], (8, 128)), 127)
    slots = jnp.zeros((8, 128), jnp.int32)
    for slot in range(128):
        slots = jnp.where(order == map_s[0, slot], slot, slots)
    lines = [slots] + [pick(jnp.broadcast_to(anchors_v[which : which + 1, :], (8, 128)), order) for which in range(2)]
    for index, line in enumerate(lines):
        notes_v[index : index + 1, :] = line[0:1]
    note_copy = pltpu.make_async_copy(notes_v, notes, in_sem.at[0])
    note_copy.start()
    brick_id = jnp.bitwise_and(map_s[0, layer * PLANE + screen], 127)
    row0, col0 = anchors_s[0, brick_id], anchors_s[1, brick_id]
    first_row, end_row = rects_s[0, brick_id], rects_s[1, brick_id]
    first_col, end_col = rects_s[2, brick_id], rects_s[3, brick_id]

    lower, upper = [], []
    for which in range(4):
        line = color_v[which : which + 1, :] if which < 3 else extinct_v[...]
        line = jnp.broadcast_to(line.astype(jnp.float32), (16, 128))
        lower.append(line.astype(jnp.bfloat16))
        upper.append(pltpu.roll(line, 127, 1).astype(jnp.bfloat16))
    row_index = lax.broadcasted_iota(jnp.int32, (16, 128), 0)
    col_index = lax.broadcasted_iota(jnp.int32, (16, 128), 1)
    col_inside = (col_index >= first_col) & (col_index < end_col)
    blank = jnp.zeros((16, 128), jnp.float32)
    turn = jnp.bitwise_and(col0, 127)
    def render(stage, near, waits):
        owner0 = (z // 2 if near else 1 - z // 2) * 16
        start = jnp.bitwise_and(stage * PLANE + owner0 - row0, 127)
        depth, clear, sums = blank, blank + 1.0, [blank] * 3
        for sample in range(SAMPLES):
            if sample % CHUNK == 0:
                for copy in waits[sample // CHUNK * 2 : sample // CHUNK * 2 + 2]:
                    copy.wait()
            position = field_v[sample // CHUNK][sample % CHUNK, pl.ds(start, 16), :] * 127.0
            knot = jnp.floor(position)
            part = position - knot
            lanes = jnp.bitwise_and(knot.astype(jnp.int32).astype(jnp.int16), jnp.int16(127))
            low = (1.0 - part).astype(jnp.bfloat16).astype(jnp.float32)
            up = part.astype(jnp.bfloat16).astype(jnp.float32)
            below = [pick(table, lanes).astype(jnp.float32) for table in lower]
            above = [pick(table, lanes).astype(jnp.float32) for table in upper]
            depth = depth - (below[3] * low + above[3] * up)
            behind = jnp.exp(depth)
            weight = clear - behind
            clear = behind
            low, up = low * weight, up * weight
            sums = [sums[which] + (below[which] * low + above[which] * up) for which in range(3)]
        row = jnp.bitwise_and(row_index + start, 127)
        inside = col_inside & (row >= first_row) & (row < end_row)
        for which, total in enumerate([*sums, 1.0 - clear]):
            total = pltpu.roll(jnp.where(inside, total, 0.0), turn, 1)
            rows[stage, which, pl.ds(pl.multiple_of(owner0, 16), 16), :] = total

    def send(stage, near):
        owner0 = (z // 2 if near else 1 - z // 2) * 16
        for index in range(16):
            peer = owner0 + lax.rem(screen + index, 16)
            if near and index == 0:
                pltpu.make_async_copy(rows.at[stage, :, pl.ds(screen, 1)], parts[stage].at[screen], a2a_recv.at[stage]).start()
            else:
                pltpu.make_async_remote_copy(
                    rows.at[stage, :, pl.ds(peer, 1)], parts[stage].at[screen], a2a_send.at[stage], a2a_recv.at[stage],
                    device_id={"screen": peer},
                ).start()

    turns = [(0, False), (1, False), (0, True), (2, False), (1, True), (3, False), (2, True), (3, True)]
    for index, now in enumerate(turns):
        if index == 2:
            pl.semaphore_wait(barrier, greetings)
            for earlier in turns[:index - 1]:
                send(*earlier)
        if index >= 2:
            send(*turns[index - 1])
        render(*now, big if index == 0 else [])
    send(*turns[-1])

    note_copy.wait()
    places = [jnp.bitwise_and(jnp.right_shift(notes[0, place * PLANE], 5), 3) for place in range(4)]
    base = jnp.int32(0)
    for place in range(4):
        base = jnp.where(places[place] == layer, place * PLANE, base)
    def all_of(ref, sem):
        pltpu.make_async_copy(ref, ref, sem).wait()

    def composite(stage):
        row_class = stage * PLANE + screen
        all_of(parts[stage], a2a_recv.at[stage])

        def brick(index, state):
            clear, sums = state
            source = jnp.bitwise_and(notes[0, base + index], PLANE - 1)
            row_at, col_at = notes[1, base + index], notes[2, base + index]
            block = jnp.right_shift(row_at - row_class + 127, 7)
            column = jnp.right_shift(col_at, 7) + jnp.where(lane < jnp.bitwise_and(col_at, 127), 1, 0)
            key = block * 8 + column - sub
            comps = [
                jnp.broadcast_to(parts[stage][source, which], (8, 128)) for which in range(4)
            ]
            new_clear, new_sums = [], []
            for spot in range(4):
                weight = jnp.where(key == spot * 8, clear[spot], 0.0)
                new_clear.append(clear[spot] - weight * comps[3])
                new_sums.append([sums[spot][which] + weight * comps[which] for which in range(3)])
            return new_clear, new_sums

        clear, sums = lax.fori_loop(
            0, PLANE, brick, ([zero + 1.0] * 4, [[zero] * 3 for _ in range(4)]), unroll=8
        )
        for spot in range(4):
            for which in range(4):
                value = sums[spot][which] if which < 3 else 1.0 - clear[spot]
                for strip in range(4):
                    layer_send[stage, strip, spot, which] = value[strip * 2 : strip * 2 + 2]
        for step in (2, 1, 3, 0):
            strip = wrap(layer + step)
            for turned in range(2):
                side = lax.rem(core + turned, 2)
                source, target = layer_send.at[stage, strip, pl.ds(side * 2, 2)], layers[stage].at[layer, core]
                if step or turned:
                    pltpu.make_async_remote_copy(
                        source, target, y_send.at[stage], y_recv.at[stage],
                        device_id={"depth": strip, "screen": chip * 2 + side},
                    ).start()
                else:
                    pltpu.make_async_copy(source, target, y_recv.at[stage]).start()

    def spot_of(first, second):
        dz = jnp.where(core == 0, second, first)
        dx = jnp.where(core == 0, first, second)
        return wrap(z + dz) * 4 + wrap(x + dx)

    def tile(stage, first, second):
        spot = spot_of(first, second)
        lines = pl.ds(pl.multiple_of(lax.rem(spot, 4) * 2, 2), 2)
        return out.at[:, pl.ds(core * 2, 2), stage * 4 + spot // 4, lines]

    def push(stage, first, second, recv, target, send):
        region = tile(stage, first, second)
        copy = pltpu.make_async_remote_copy(region, region, send, recv, device_id=target)
        copy.start()
        return copy

    def landed(sem):
        piece = out.at[:, pl.ds(0, 2), 0, pl.ds(0, 2)]
        pltpu.make_async_copy(piece, piece, sem).wait()

    def to_twin(stage, gone):
        region = out.at[:, pl.ds(core * 2, 2), stage * 4 + wrap(z - gone)]
        pltpu.make_async_remote_copy(region, region, twin_send, twin_recv, device_id=twin).start()

    def second_phase(stage, gone):
        for step in (1, 3, 2):
            push(
                stage, -gone, 0, second_recv.at[stage, gone, step], {"screen": spot_of(0, step) * 2 + core}, tile_send
            )

    def finish(stage):
        all_of(layers[stage], y_recv.at[stage])
        values = []
        for spot in range(2):
            sides = []
            for source in range(2):
                clear, sums = jnp.ones((2, 128), jnp.float32), [jnp.zeros((2, 128), jnp.float32)] * 3
                for place in range(4):
                    one = places[place]
                    sums = [sums[which] + clear * layers[stage][one, source, spot, which] for which in range(3)]
                    clear = clear - clear * layers[stage][one, source, spot, 3]
                sides.append([*sums, 1.0 - clear])
            values.append([
                [jnp.concatenate([one[which][side : side + 1] for one in sides], axis=0) for side in range(2)]
                for which in range(4)
            ])
        for turned in range(4):
            @pl.when(lax.rem(chip, 4) == turned)
            def _():
                for spot in range(2):
                    for which in range(4):
                        for side in range(2):
                            out[
                                which, core * 2 + spot, stage * 4 + z, turned * 2 : turned * 2 + 2,
                                side * 128 : side * 128 + 128,
                            ] = values[spot][which][side]

        for step in (1, 3, 2):
            push(stage, 0, 0, first_recv.at[stage, step], {"screen": spot_of(step, 0) * 2 + core}, tile_send)
        second_phase(stage, 0)

    def forward(stage):
        for step in (1, 3, 2):
            landed(first_recv.at[stage, step])
            second_phase(stage, step)

    def collect(stage):
        @pl.when(core == 0)
        def _():
            to_twin(stage, 0)
            for step in (1, 3, 2):
                for gone in (0, 1, 3, 2):
                    landed(second_recv.at[stage, gone, step])
                to_twin(stage, step)

        @pl.when(core == 1)
        def _():
            for gone in (0, 1, 3, 2):
                for step in (1, 3, 2):
                    landed(second_recv.at[stage, gone, step])
                to_twin(stage, gone)

    for work in (composite, finish, forward, collect):
        for stage in range(STAGES):
            work(stage)
    all_of(out.at[:, pl.ds(0, 2)], twin_recv)
    all_of(out.at[:, pl.ds(0, 2)], twin_send)
    all_of(out.at[:, pl.ds(0, 2), pl.ds(0, 15)], tile_send)
    for stage in range(STAGES):
        all_of(rows.at[stage, :, pl.ds(0, PLANE - 1)], a2a_send.at[stage])
        all_of(layers[stage].at[pl.ds(0, 3)], y_send.at[stage])
        all_of(layers[stage].at[0, 0], y_send.at[stage])


def shards(brick_field, tf_color, tf_extinction, brick_map, view_order, anchors, rects):
    out = pl.pallas_call(
        frame_kernel,
        out_shape=pltpu.VMEM((4, 4, 16, 8, 256), jnp.float32),
        in_specs=[HBM] * 7,
        out_specs=VMEM,
        scratch_shapes=[
            pltpu.VMEM((1, 128), jnp.int32), pltpu.VMEM((1, 128), jnp.int32), pltpu.VMEM((2, 128), jnp.int32),
            pltpu.VMEM((3, 128), jnp.bfloat16), pltpu.VMEM((1, 128), jnp.bfloat16),
            pltpu.SMEM((1, 128), jnp.int32), pltpu.SMEM((2, 128), jnp.int32), pltpu.SMEM((4, 128), jnp.int32),
            pltpu.VMEM((8, 128), jnp.int32), pltpu.SMEM((8, 128), jnp.int32),
            tuple(pltpu.VMEM((CHUNK, 144, 128), jnp.float32) for _ in range(SAMPLES // CHUNK)),
            pltpu.VMEM((STAGES, 4, PLANE, 128), jnp.float32),
            tuple(pltpu.VMEM((PLANE, 4, 1, 128), jnp.float32) for _ in range(STAGES)),
            pltpu.VMEM((STAGES, 4, 4, 4, 2, 128), jnp.float32),
            tuple(pltpu.VMEM((4, 2, 2, 4, 2, 128), jnp.float32) for _ in range(STAGES)),
            DMA((8,)), DMA((SAMPLES // CHUNK, 2)), DMA((STAGES,)), DMA((STAGES,)), DMA((STAGES,)), DMA((STAGES,)),
            DMA(()), DMA((STAGES, 4)), DMA((STAGES, 4, 4)), DMA(()), DMA(()),
        ],
        compiler_params=pltpu.CompilerParams(
            collective_id=0, has_side_effects=True, vmem_limit_bytes=56 * 2**20
        ),
        name="frame",
    )(
        brick_map.reshape(1, 128), view_order.reshape(1, 128), anchors.T, rects.T,
        brick_field, tf_color, tf_extinction.reshape(1, 128),
    )
    return out.reshape(4, 512, 256)


def solution(mesh):
    placed = (P("depth", "screen", None, None, None), P(), P(), P(), P(), P(), P())
    return jax.shard_map(
        shards, mesh=mesh, in_specs=placed, out_specs=P(None, None, "depth"), check_vma=False
    )
```

```python
import jax
import jax.numpy as jnp
from jax import lax
from jax.experimental import pallas as pl
from jax.experimental.pallas import tpu as pltpu
from jax.sharding import PartitionSpec as P

DMA = pltpu.SemaphoreType.DMA
HBM = pl.BlockSpec(memory_space=pltpu.HBM)
VMEM = pl.BlockSpec(memory_space=pltpu.VMEM)
SAMPLES = 32
CHUNK = SAMPLES
PLANE = 32
STAGES = 4
PICK = lax.GatherDimensionNumbers(
    offset_dims=(), collapsed_slice_dims=(1,), start_index_map=(1,),
    operand_batching_dims=(0,), start_indices_batching_dims=(0,),
)


def pick(table, lanes):
    return lax.gather(table, lanes[..., None], PICK, (1, 1), mode=lax.GatherScatterMode.PROMISE_IN_BOUNDS)


def wrap(value):
    return lax.rem(value + 8, 4)


def frame_kernel(
    brick_map, view_order, anchors, rects, field, color, extinct, out,
    map_v, order_v, anchors_v, color_v, extinct_v, map_s, anchors_s, rects_s, notes_v, notes, field_v,
    rows, parts, layer_send, layers,
    in_sem, field_sem, a2a_send, a2a_recv, y_send, y_recv,
    tile_send, first_recv, second_recv, twin_send, twin_recv,
):
    layer, screen = lax.axis_index("depth"), lax.axis_index("screen")
    z, x, core = screen // 8, lax.rem(screen // 2, 4), lax.rem(screen, 2)
    chip = screen // 2
    twin = {"screen": chip * 2 + 1 - core}

    small = [
        pltpu.make_async_copy(source, target, in_sem.at[index])
        for index, (source, target) in enumerate([
            (brick_map, map_s), (anchors, anchors_s), (rects, rects_s), (color, color_v), (extinct, extinct_v),
            (brick_map, map_v), (view_order, order_v), (anchors, anchors_v),
        ])
    ]
    big = [
        pltpu.make_async_copy(
            field.at[0, 0, pl.ds(chunk * CHUNK, CHUNK), pl.ds(0, lines)],
            field_v[chunk].at[:, pl.ds(at, lines)], field_sem.at[chunk, part],
        )
        for chunk in range(SAMPLES // CHUNK) for part, (at, lines) in enumerate(((0, 128), (128, 16)))
    ]
    for copy in small + big:
        copy.start()

    barrier = pltpu.get_barrier_semaphore()

    def greet(step, carry):
        pl.semaphore_signal(barrier, inc=1, device_id={"screen": lax.rem(screen + step, PLANE)})
        return carry

    lax.fori_loop(1, PLANE, greet, 0)
    for step in (1, 2, 3):
        for index in range(2):
            pl.semaphore_signal(barrier, inc=1, device_id={"depth": wrap(layer + step), "screen": chip * 2 + index})
    greetings = PLANE - 1 + 6

    sub = lax.broadcasted_iota(jnp.int32, (8, 128), 0)
    lane = lax.broadcasted_iota(jnp.int32, (8, 128), 1)
    zero = jnp.zeros((8, 128), jnp.float32)

    for copy in small:
        copy.wait()
    order = jnp.bitwise_and(jnp.broadcast_to(order_v[...], (8, 128)), 127)
    slots = jnp.zeros((8, 128), jnp.int32)
    for slot in range(128):
        slots = jnp.where(order == map_s[0, slot], slot, slots)
    lines = [slots] + [pick(jnp.broadcast_to(anchors_v[which : which + 1, :], (8, 128)), order) for which in range(2)]
    for index, line in enumerate(lines):
        notes_v[index : index + 1, :] = line[0:1]
    note_copy = pltpu.make_async_copy(notes_v, notes, in_sem.at[0])
    note_copy.start()
    brick_id = jnp.bitwise_and(map_s[0, layer * PLANE + screen], 127)
    row0, col0 = anchors_s[0, brick_id], anchors_s[1, brick_id]
    first_row, end_row = rects_s[0, brick_id], rects_s[1, brick_id]
    first_col, end_col = rects_s[2, brick_id], rects_s[3, brick_id]

    lower, upper = [], []
    for which in range(4):
        line = color_v[which : which + 1, :] if which < 3 else extinct_v[...]
        line = jnp.broadcast_to(line.astype(jnp.float32), (16, 128))
        lower.append(line.astype(jnp.bfloat16))
        upper.append(pltpu.roll(line, 127, 1).astype(jnp.bfloat16))
    row_index = lax.broadcasted_iota(jnp.int32, (16, 128), 0)
    col_index = lax.broadcasted_iota(jnp.int32, (16, 128), 1)
    col_inside = (col_index >= first_col) & (col_index < end_col)
    blank = jnp.zeros((16, 128), jnp.float32)
    turn = jnp.bitwise_and(col0, 127)
    def render(stage, near, waits):
        owner0 = (z // 2 if near else 1 - z // 2) * 16
        start = jnp.bitwise_and(stage * PLANE + owner0 - row0, 127)
        depth, clear, sums = blank, blank + 1.0, [blank] * 3
        for sample in range(SAMPLES):
            if sample % CHUNK == 0:
                for copy in waits[sample // CHUNK * 2 : sample // CHUNK * 2 + 2]:
                    copy.wait()
            position = field_v[sample // CHUNK][sample % CHUNK, pl.ds(start, 16), :] * 127.0
            knot = jnp.floor(position)
            part = position - knot
            lanes = jnp.bitwise_and(knot.astype(jnp.int32).astype(jnp.int16), jnp.int16(127))
            low = (1.0 - part).astype(jnp.bfloat16).astype(jnp.float32)
            up = part.astype(jnp.bfloat16).astype(jnp.float32)
            below = [pick(table, lanes).astype(jnp.float32) for table in lower]
            above = [pick(table, lanes).astype(jnp.float32) for table in upper]
            depth = depth - (below[3] * low + above[3] * up)
            behind = jnp.exp(depth)
            weight = clear - behind
            clear = behind
            low, up = low * weight, up * weight
            sums = [sums[which] + (below[which] * low + above[which] * up) for which in range(3)]
        row = jnp.bitwise_and(row_index + start, 127)
        inside = col_inside & (row >= first_row) & (row < end_row)
        for which, total in enumerate([*sums, 1.0 - clear]):
            total = pltpu.roll(jnp.where(inside, total, 0.0), turn, 1)
            rows[stage, which, pl.ds(pl.multiple_of(owner0, 16), 16), :] = total

    def send(stage, near):
        owner0 = (z // 2 if near else 1 - z // 2) * 16
        for index in range(16):
            peer = owner0 + lax.rem(screen + index, 16)
            if near and index == 0:
                pltpu.make_async_copy(rows.at[stage, :, pl.ds(screen, 1)], parts[stage].at[screen], a2a_recv.at[stage]).start()
            else:
                pltpu.make_async_remote_copy(
                    rows.at[stage, :, pl.ds(peer, 1)], parts[stage].at[screen], a2a_send.at[stage], a2a_recv.at[stage],
                    device_id={"screen": peer},
                ).start()

    turns = [(0, False), (1, False), (0, True), (2, False), (1, True), (3, False), (2, True), (3, True)]
    for index, now in enumerate(turns):
        if index == 2:
            pl.semaphore_wait(barrier, greetings)
            for earlier in turns[:index - 1]:
                send(*earlier)
        if index >= 2:
            send(*turns[index - 1])
        render(*now, big if index == 0 else [])
    send(*turns[-1])

    note_copy.wait()
    places = [jnp.bitwise_and(jnp.right_shift(notes[0, place * PLANE], 5), 3) for place in range(4)]
    base = jnp.int32(0)
    for place in range(4):
        base = jnp.where(places[place] == layer, place * PLANE, base)
    def all_of(ref, sem):
        pltpu.make_async_copy(ref, ref, sem).wait()

    def composite(stage):
        row_class = stage * PLANE + screen
        all_of(parts[stage], a2a_recv.at[stage])

        def brick(index, state):
            clear, sums = state
            source = jnp.bitwise_and(notes[0, base + index], PLANE - 1)
            row_at, col_at = notes[1, base + index], notes[2, base + index]
            block = jnp.right_shift(row_at - row_class + 127, 7)
            column = jnp.right_shift(col_at, 7) + jnp.where(lane < jnp.bitwise_and(col_at, 127), 1, 0)
            key = block * 8 + column - sub
            comps = [
                jnp.broadcast_to(parts[stage][source, which], (8, 128)) for which in range(4)
            ]
            new_clear, new_sums = [], []
            for spot in range(4):
                weight = jnp.where(key == spot * 8, clear[spot], 0.0)
                new_clear.append(clear[spot] - weight * comps[3])
                new_sums.append([sums[spot][which] + weight * comps[which] for which in range(3)])
            return new_clear, new_sums

        clear, sums = lax.fori_loop(
            0, PLANE, brick, ([zero + 1.0] * 4, [[zero] * 3 for _ in range(4)]), unroll=8
        )
        for spot in range(4):
            for which in range(4):
                value = sums[spot][which] if which < 3 else 1.0 - clear[spot]
                for strip in range(4):
                    layer_send[stage, strip, spot, which] = value[strip * 2 : strip * 2 + 2]
        for step in (2, 1, 3, 0):
            strip = wrap(layer + step)
            for turned in range(2):
                side = lax.rem(core + turned, 2)
                source, target = layer_send.at[stage, strip, pl.ds(side * 2, 2)], layers[stage].at[layer, core]
                if step or turned:
                    pltpu.make_async_remote_copy(
                        source, target, y_send.at[stage], y_recv.at[stage],
                        device_id={"depth": strip, "screen": chip * 2 + side},
                    ).start()
                else:
                    pltpu.make_async_copy(source, target, y_recv.at[stage]).start()

    def spot_of(first, second):
        dz = jnp.where(core == 0, second, first)
        dx = jnp.where(core == 0, first, second)
        return wrap(z + dz) * 4 + wrap(x + dx)

    def tile(stage, first, second):
        spot = spot_of(first, second)
        lines = pl.ds(pl.multiple_of(lax.rem(spot, 4) * 2, 2), 2)
        return out.at[:, pl.ds(core * 2, 2), stage * 4 + spot // 4, lines]

    def push(stage, first, second, recv, target, send):
        region = tile(stage, first, second)
        copy = pltpu.make_async_remote_copy(region, region, send, recv, device_id=target)
        copy.start()
        return copy

    def landed(sem):
        piece = out.at[:, pl.ds(0, 2), 0, pl.ds(0, 2)]
        pltpu.make_async_copy(piece, piece, sem).wait()

    def to_twin(stage, gone):
        region = out.at[:, pl.ds(core * 2, 2), stage * 4 + wrap(z - gone)]
        pltpu.make_async_remote_copy(region, region, twin_send, twin_recv, device_id=twin).start()

    def second_phase(stage, gone):
        for step in (2, 1, 3):
            push(
                stage, -gone, 0, second_recv.at[stage, gone, step], {"screen": spot_of(0, step) * 2 + core}, tile_send
            )

    def finish(stage):
        all_of(layers[stage], y_recv.at[stage])
        values = []
        for spot in range(2):
            sides = []
            for source in range(2):
                clear, sums = jnp.ones((2, 128), jnp.float32), [jnp.zeros((2, 128), jnp.float32)] * 3
                for place in range(4):
                    one = places[place]
                    sums = [sums[which] + clear * layers[stage][one, source, spot, which] for which in range(3)]
                    clear = clear - clear * layers[stage][one, source, spot, 3]
                sides.append([*sums, 1.0 - clear])
            values.append([
                [jnp.concatenate([one[which][side : side + 1] for one in sides], axis=0) for side in range(2)]
                for which in range(4)
            ])
        for turned in range(4):
            @pl.when(lax.rem(chip, 4) == turned)
            def _():
                for spot in range(2):
                    for which in range(4):
                        for side in range(2):
                            out[
                                which, core * 2 + spot, stage * 4 + z, turned * 2 : turned * 2 + 2,
                                side * 128 : side * 128 + 128,
                            ] = values[spot][which][side]

        for step in (1, 3, 2):
            push(stage, 0, 0, first_recv.at[stage, step], {"screen": spot_of(step, 0) * 2 + core}, tile_send)
        second_phase(stage, 0)

    def forward(stage):
        for step in (1, 3, 2):
            landed(first_recv.at[stage, step])
            second_phase(stage, step)

    def collect(stage):
        @pl.when(core == 0)
        def _():
            to_twin(stage, 0)
            for step in (1, 3, 2):
                for gone in (0, 1, 3, 2):
                    landed(second_recv.at[stage, gone, step])
                to_twin(stage, step)

        @pl.when(core == 1)
        def _():
            for gone in (0, 1, 3, 2):
                for step in (1, 3, 2):
                    landed(second_recv.at[stage, gone, step])
                to_twin(stage, gone)

    for work in (composite, finish, forward, collect):
        for stage in range(STAGES):
            work(stage)
    all_of(out.at[:, pl.ds(0, 2)], twin_recv)
    all_of(out.at[:, pl.ds(0, 2)], twin_send)
    all_of(out.at[:, pl.ds(0, 2), pl.ds(0, 15)], tile_send)
    for stage in range(STAGES):
        all_of(rows.at[stage, :, pl.ds(0, PLANE - 1)], a2a_send.at[stage])
        all_of(layers[stage].at[pl.ds(0, 3)], y_send.at[stage])
        all_of(layers[stage].at[0, 0], y_send.at[stage])


def shards(brick_field, tf_color, tf_extinction, brick_map, view_order, anchors, rects):
    out = pl.pallas_call(
        frame_kernel,
        out_shape=pltpu.VMEM((4, 4, 16, 8, 256), jnp.float32),
        in_specs=[HBM] * 7,
        out_specs=VMEM,
        scratch_shapes=[
            pltpu.VMEM((1, 128), jnp.int32), pltpu.VMEM((1, 128), jnp.int32), pltpu.VMEM((2, 128), jnp.int32),
            pltpu.VMEM((3, 128), jnp.bfloat16), pltpu.VMEM((1, 128), jnp.bfloat16),
            pltpu.SMEM((1, 128), jnp.int32), pltpu.SMEM((2, 128), jnp.int32), pltpu.SMEM((4, 128), jnp.int32),
            pltpu.VMEM((8, 128), jnp.int32), pltpu.SMEM((8, 128), jnp.int32),
            tuple(pltpu.VMEM((CHUNK, 144, 128), jnp.float32) for _ in range(SAMPLES // CHUNK)),
            pltpu.VMEM((STAGES, 4, PLANE, 128), jnp.float32),
            tuple(pltpu.VMEM((PLANE, 4, 1, 128), jnp.float32) for _ in range(STAGES)),
            pltpu.VMEM((STAGES, 4, 4, 4, 2, 128), jnp.float32),
            tuple(pltpu.VMEM((4, 2, 2, 4, 2, 128), jnp.float32) for _ in range(STAGES)),
            DMA((8,)), DMA((SAMPLES // CHUNK, 2)), DMA((STAGES,)), DMA((STAGES,)), DMA((STAGES,)), DMA((STAGES,)),
            DMA(()), DMA((STAGES, 4)), DMA((STAGES, 4, 4)), DMA(()), DMA(()),
        ],
        compiler_params=pltpu.CompilerParams(
            collective_id=0, has_side_effects=True, vmem_limit_bytes=56 * 2**20
        ),
        name="frame",
    )(
        brick_map.reshape(1, 128), view_order.reshape(1, 128), anchors.T, rects.T,
        brick_field, tf_color, tf_extinction.reshape(1, 128),
    )
    return out.reshape(4, 512, 256)


def solution(mesh):
    placed = (P("depth", "screen", None, None, None), P(), P(), P(), P(), P(), P())
    return jax.shard_map(
        shards, mesh=mesh, in_specs=placed, out_specs=P(None, None, "depth"), check_vma=False
    )
```
